32 devices in a mesh: grp: 1, gx: 16 (over z, y, x), gy: 2 (over core).
Axes of the slice: x: 2, y: 2, z: 4, core: 2. Of those that a mesh axis runs over, the one named last changes fastest.
Arguments:
- log_conf: bfloat16 [6, 64, 512, 128], P(None, ('grp', 'gx'), 'gy'), may hold values from -3 to 3
- brownian: bfloat16 [6, 64, 512, 128], P(None, ('grp', 'gx'), 'gy'), may hold values from -6 to 6
- relax_rate: bfloat16 [64, 512, 128], P(('grp', 'gx'), 'gy'), may hold values from 0.5 to 5
- kernel: float32 [6, 5, 5, 5], replicated, may hold values from -0.5 to 0.5
Outputs:
- downsampled_stress: float32 [6, 32, 16, 128], P(None, ('gx', 'gy'), 'grp')
The draws below stay inside these ranges and needn't reach their ends.
All inputs are finite; a program needn't handle non-finite values.
Results may differ from the reference program's by a relative error of at most 0.0003.
Values may be sent and summed in bfloat16 or wider, within the bound.
No kernel may reach another device: no remote copies, remote signals or barrier semaphores. Data moves between devices by JAX's collectives and lax.ppermute only.
A program may use at most 128 MiB of HBM per device.

```python
import math
import jax
import jax.numpy as jnp
from jax import lax

NC = 6
NX = 64
NY = 512
NZ = 128


def block_levels(stream_key, shape, pieces, smallest, largest):
    def one(dim, blocks):
        heights = jax.random.uniform(jax.random.fold_in(jax.random.fold_in(stream_key, 6), dim), (blocks,), jnp.float32, smallest / len(pieces), largest / len(pieces))
        return jnp.repeat(jnp.exp(heights), shape[dim] // blocks).reshape((-1,) + (1,) * (len(shape) - dim - 1))

    loudness = one(*pieces[0])
    for cut in pieces[1:]:
        loudness = loudness * one(*cut)
    return loudness


def normal_values(key, extent, deviation, most, split=(), held_as=jnp.bfloat16):
    drawn = jax.random.normal(key, extent, jnp.float32) * deviation
    if len(split) > 0:
        drawn = block_levels(key, extent, split, -0.22, 0.18) * drawn
    return jnp.clip(drawn, min=-most, max=most).astype(held_as)


def setup_inputs(seed: int = 0, part: int = 0) -> dict:
    splits = jax.random.split(jax.random.key(seed), 5)
    own_keys = jax.random.split(jax.random.fold_in(splits[4], part), 5)
    return {
        "log_conf": normal_values(own_keys[0], (NC, NX, NY, NZ), 0.5, 3.0, ((1, 16), (2, 2))),
        "brownian": normal_values(own_keys[1], (NC, NX, NY, NZ), 1.0, 6.0, ((1, 16), (2, 2))),
        "relax_rate": jnp.clip(jnp.exp(math.log(5.0) - 2.3025851 * jax.random.uniform(own_keys[2], (NX, NY, NZ), jnp.float32) ** block_levels(own_keys[2], (NX, NY, NZ), ((0, 16), (1, 2)), -0.2, 0.2)), 0.5, 5.0).astype(jnp.bfloat16),
        "kernel": normal_values(splits[3], (NC, 5, 5, 5), 125 ** -0.5, 0.5, (), jnp.float32),
    }


DIFFUSE = 0.12
RELAX_STEP = 0.1
NOISE_AMP = 0.3


def window(padded, axis, start):
    result = padded
    for dim in (1, 2, 3):
        length = padded.shape[dim] - 4
        begin = start if dim == axis else 2
        result = lax.slice_in_dim(result, begin, begin + length, axis=dim)
    return result


def diffusion_operator(padded):
    total = jnp.zeros_like(window(padded, 1, 2))
    for axis in (1, 2, 3):
        total = total + (-window(padded, axis, 0) + 16.0 * window(padded, axis, 1) - 30.0 * window(padded, axis, 2)
                         + 16.0 * window(padded, axis, 3) - window(padded, axis, 4)) / 12.0
    return total


def second_order(field):
    comp_xx, comp_xy, comp_xz, comp_yy, comp_yz, comp_zz = [field[comp_index] for comp_index in range(6)]
    squared_values = jnp.stack([
        comp_xx * comp_xx + comp_xy * comp_xy + comp_xz * comp_xz,
        comp_xx * comp_xy + comp_xy * comp_yy + comp_xz * comp_yz,
        comp_xx * comp_xz + comp_xy * comp_yz + comp_xz * comp_zz,
        comp_xy * comp_xy + comp_yy * comp_yy + comp_yz * comp_yz,
        comp_xy * comp_xz + comp_yy * comp_yz + comp_yz * comp_zz,
        comp_xz * comp_xz + comp_yz * comp_yz + comp_zz * comp_zz])
    return field + 0.5 * squared_values


def reference(log_conf, brownian, relax_rate, kernel):
    field = log_conf.astype(jnp.float32)
    padded = jnp.pad(field, ((0, 0), (2, 2), (2, 2), (2, 2)))
    lap = diffusion_operator(padded)
    updated = field + DIFFUSE * lap - RELAX_STEP * relax_rate.astype(jnp.float32)[None] * field + NOISE_AMP * brownian.astype(jnp.float32)
    stress = second_order(updated)
    stress_pad = jnp.pad(stress, ((0, 0), (2, 2), (2, 2), (2, 2)))
    downsampled = lax.conv_general_dilated(stress_pad[None], kernel.astype(jnp.float32)[:, None], (4, 4, 4), "VALID",
                                      dimension_numbers=("NCDHW", "OIDHW", "NCDHW"), feature_group_count=6,
                                      precision=lax.Precision.HIGHEST)[0]
    return jnp.transpose(downsampled, (0, 3, 1, 2))
```

```python
import functools

import jax
import jax.numpy as jnp
from jax import lax
from jax.experimental import pallas as pl
from jax.experimental.pallas import tpu as pltpu
from jax.sharding import PartitionSpec as P

STENCIL = 0.12 / 12.0
RELAX_STEP = 0.1
NOISE_AMP = 0.3
NC = 6
LANES = 128
LEAD = 8
TAIL = 32


def band(size):
    row = lax.broadcasted_iota(jnp.int32, (size, size), 0)
    col = lax.broadcasted_iota(jnp.int32, (size, size), 1)
    gap = jnp.abs(row - col)
    value = jnp.where(gap == 0, -30.0, jnp.where(gap == 1, 16.0, jnp.where(gap == 2, -1.0, 0.0)))
    return value.astype(jnp.bfloat16)


def begin_kernel(idx_ref, f_ref, b_ref, r_ref, cols_ref, ty_ref, tz_ref, out_ref):
    rows, ny = f_ref.shape[1], f_ref.shape[2]
    odd, gy = idx_ref[0], idx_ref[1]
    step = 64
    for x in range(rows):
        side = jnp.where(odd == 1, x // 2, 1 - x // 2)
        plane = f_ref[0, x]
        for y in range(0, ny, step):
            ys = pl.ds(y, step)
            part = f_ref[0, x, ys]
            lap = jnp.dot(ty_ref[ys], plane, preferred_element_type=jnp.float32)
            lap += jnp.dot(part, tz_ref[...], preferred_element_type=jnp.float32)
            own = part.astype(jnp.float32)
            lap -= 30.0 * own
            for other in range(rows):
                if abs(other - x) == 1:
                    lap += 16.0 * f_ref[0, other, ys].astype(jnp.float32)
                elif abs(other - x) == 2:
                    lap -= f_ref[0, other, ys].astype(jnp.float32)
            rate = r_ref[x, ys].astype(jnp.float32)
            noise = b_ref[0, x, ys].astype(jnp.float32)
            out_ref[side, 0, x % 2, ys] = own - RELAX_STEP * rate * own + NOISE_AMP * noise + STENCIL * lap
        near_row = lax.broadcasted_iota(jnp.int32, (8, 1), 0)
        first = cols_ref[0, x, 0:1]
        second = cols_ref[0, x, 1:2]

        @pl.when(gy == 1)
        def _():
            extra = jnp.where(near_row == 0, 16.0 * second - first, jnp.where(near_row == 1, -second, 0.0))
            out_ref[side, 0, x % 2, 0:8] += STENCIL * extra

        @pl.when(gy == 0)
        def _():
            extra = jnp.where(near_row == 7, 16.0 * first - second, jnp.where(near_row == 6, -first, 0.0))
            out_ref[side, 0, x % 2, ny - 8 : ny] += STENCIL * extra


def begin(idx, log_conf, brownian, relax_rate, cols):
    comps, rows, ny, nz = log_conf.shape
    whole = lambda *shape: pl.BlockSpec(shape, lambda c: (0,) * len(shape))
    block = pl.BlockSpec((1, rows, ny, nz), lambda c: (c, 0, 0, 0))
    return pl.pallas_call(
        begin_kernel,
        grid=(comps,),
        in_specs=[
            pl.BlockSpec(memory_space=pltpu.SMEM),
            block,
            block,
            whole(rows, ny, nz),
            pl.BlockSpec((1, rows, 2, nz), lambda c: (c, 0, 0, 0)),
            whole(ny, ny),
            whole(nz, nz),
        ],
        out_specs=pl.BlockSpec((2, 1, 2, ny, nz), lambda c: (0, c, 0, 0, 0)),
        out_shape=jax.ShapeDtypeStruct((2, comps, 2, ny, nz), jnp.float32),
        compiler_params=pltpu.CompilerParams(vmem_limit_bytes=24 * 2**20),
        cost_estimate=pl.CostEstimate(
            flops=30 * comps * rows * ny * nz, bytes_accessed=10 * comps * rows * ny * nz, transcendentals=0
        ),
        name="begin",
    )(idx, log_conf, brownian, relax_rate, cols, band(ny), band(nz))


def finish_kernel(side, has_base, idx_ref, u_ref, halo_ref, w_ref, pick_ref, *refs):
    if has_base:
        base_ref, out_ref, stress, sums = refs
    else:
        out_ref, stress, sums = refs
    ny, nz = u_ref.shape[3], u_ref.shape[4]
    nj = ny // 4
    planes = out_ref.shape[0] // 8
    odd = idx_ref[0]
    upper = (odd == side).astype(jnp.int32)
    near, far = 1 - upper, upper
    edge, inner = upper, 1 - upper
    for c in range(NC):
        for r in range(2):
            for piece in range(nz // LANES):
                stress[c, r, piece, 0:LEAD] = jnp.zeros((LEAD, LANES), jnp.float32)
                stress[c, r, piece, LEAD + ny : LEAD + ny + TAIL] = jnp.zeros((TAIL, LANES), jnp.float32)

    def chunk(step, carry):
        y = pl.multiple_of(step * 16, 16)
        ys = pl.ds(y, 16)
        rows = ([], [])
        for c in range(NC):
            close = halo_ref[c, near, ys].astype(jnp.float32)
            distant = halo_ref[c, far, ys].astype(jnp.float32)
            rows[0].append(u_ref[0, c, inner, ys] - STENCIL * close)
            rows[1].append(u_ref[0, c, edge, ys] + (16.0 * STENCIL) * close - STENCIL * distant)
        for r in range(2):
            xx, xy, xz, yy, yz, zz = rows[r]
            xy2, xz2, yz2 = xy * xy, xz * xz, yz * yz
            values = (
                xx + 0.5 * (xx * xx + xy2 + xz2),
                xy + 0.5 * (xy * (xx + yy) + xz * yz),
                xz + 0.5 * (xz * (xx + zz) + xy * yz),
                yy + 0.5 * (xy2 + yy * yy + yz2),
                yz + 0.5 * (yz * (yy + zz) + xy * xz),
                zz + 0.5 * (xz2 + yz2 + zz * zz),
            )
            for c in range(NC):
                for piece in range(nz // LANES):
                    stress[c, r, piece, pl.ds(y + LEAD, 16)] = values[c][:, piece * LANES : (piece + 1) * LANES]
        return carry

    lax.fori_loop(0, ny // 16, chunk, 0)

    main_i = jnp.where(upper == 1, 0, 3)
    main_e = jnp.where(upper == 1, 1, 2)
    extra_i = jnp.where(upper == 1, 4, 5)
    height = nj + 8
    main_at = pl.multiple_of(upper * height, 8)
    extra_at = pl.multiple_of((1 - upper) * height, 8)
    for c in range(NC):
        weight = {}
        for b in range(5):
            for k in range(2):
                for name, a in (("mi", main_i), ("me", main_e), ("xi", extra_i)):
                    weight[name, b, k] = w_ref[c, a, 2 * b + k : 2 * b + k + 1]
        for jb in range(nj // 8 + 1):
            main = [None, None]
            extra = [None, None]
            for b in range(5 if jb < nj // 8 else 2):
                at = pl.ds(LEAD + 32 * jb + b - 2, 8, stride=4)
                inside = jnp.concatenate([stress[c, 0, piece, at] for piece in range(nz // LANES)], axis=1)
                outside = jnp.concatenate([stress[c, 1, piece, at] for piece in range(nz // LANES)], axis=1)
                for k in range(2):
                    term = inside * weight["mi", b, k] + outside * weight["me", b, k]
                    main[k] = term if main[k] is None else main[k] + term
                    term = inside * weight["xi", b, k]
                    extra[k] = term if extra[k] is None else extra[k] + term
            for k in range(2):
                sums[c, pl.ds(main_at + 8 * jb, 8), k * nz : (k + 1) * nz] = main[k]
                sums[c, pl.ds(extra_at + 8 * jb, 8), k * nz : (k + 1) * nz] = extra[k]

    def reduced(values):
        high = values.astype(jnp.bfloat16)
        low = (values - high.astype(jnp.float32)).astype(jnp.bfloat16)
        both = jnp.concatenate([high, low], axis=1)
        return lax.dot_general(
            pick_ref[...], both, (((1,), (1,)), ((), ())), preferred_element_type=jnp.float32
        )

    def put(place, value):
        rows = pl.ds(place, planes, stride=8)
        if has_base:
            value = value + base_ref[rows, :]
        out_ref[rows, :] = value

    for c in range(NC):
        put(c, reduced(jnp.concatenate([sums[c, 0:nj], sums[c, height : height + nj]], axis=0)))
    beyond = []
    for c in range(NC):
        for t in range(2):
            beyond.append(sums[c, t * height + nj : t * height + nj + 1])
    beyond.append(jnp.zeros((2 * nj - 2 * NC, 2 * nz), jnp.float32))
    put(NC, reduced(jnp.concatenate(beyond, axis=0)))
    out_ref[pl.ds(7, planes, stride=8), :] = jnp.zeros((planes, 2 * nj), jnp.float32)


def finish(side, idx, begun, halo, weights, pick, base):
    _, comps, _, ny, nz = begun.shape
    planes, nj = nz // 4, ny // 4
    vmem = pl.BlockSpec(memory_space=pltpu.VMEM)
    operands = [idx, begun, halo, weights, pick] + ([] if base is None else [base])
    specs = [
        pl.BlockSpec(memory_space=pltpu.SMEM),
        pl.BlockSpec((1, comps, 2, ny, nz), lambda i: (side, 0, 0, 0, 0)),
    ] + [pl.BlockSpec(x.shape, functools.partial(lambda n, i: (0,) * n, x.ndim)) for x in operands[2:]]
    return pl.pallas_call(
        functools.partial(finish_kernel, side, base is not None),
        grid=(1,),
        in_specs=specs,
        out_specs=pl.BlockSpec((planes * 8, 2 * nj), lambda i: (0, 0)),
        out_shape=jax.ShapeDtypeStruct((planes * 8, 2 * nj), jnp.float32),
        scratch_shapes=[
            pltpu.VMEM((comps, 2, nz // LANES, LEAD + ny + TAIL, LANES), jnp.float32),
            pltpu.VMEM((comps, 2 * (nj + 8), 2 * nz), jnp.float32),
        ],
        compiler_params=pltpu.CompilerParams(vmem_limit_bytes=32 * 2**20),
        cost_estimate=pl.CostEstimate(
            flops=40 * comps * ny * nz, bytes_accessed=16 * comps * ny * nz, transcendentals=0
        ),
        name="finish",
    )(*operands)


def gather_kernel(in_ref, out_ref):
    count, lanes = out_ref.shape[2], out_ref.shape[3]
    half = lanes // 2
    lane = lax.broadcasted_iota(jnp.int32, (count, lanes), 1)
    row = lax.broadcasted_iota(jnp.int32, (count, lanes), 0)
    low = lane < half
    beyond = in_ref[pl.ds(NC, count, stride=16), :]
    for c in range(NC):
        first = in_ref[pl.ds(c, count, stride=16), :]
        second = in_ref[pl.ds(8 + c, count, stride=16), :]
        own = jnp.where(low, first, pltpu.roll(second, half, 1))
        own += jnp.where(lane == half, pltpu.roll(beyond, half - 2 * c, 1), 0.0)
        after = jnp.where(low, pltpu.roll(first, half, 1), second)
        after += jnp.where(lane == half, pltpu.roll(beyond, half - 2 * c - 1, 1), 0.0)
        out_ref[c, 0] = own + jnp.where(row > 0, pltpu.roll(after, 1, 0), 0.0)


def local(log_conf, brownian, relax_rate, kernel):
    comps, rows, ny, nz = log_conf.shape
    width_gx, width_gy = lax.axis_size("gx"), lax.axis_size("gy")
    planes = nz // 4
    assert comps == NC and rows == 4 and width_gy == 2 and width_gx % 2 == 0
    assert planes == width_gx * width_gy
    odd = lax.axis_index("gx") % 2
    gy = lax.axis_index("gy")

    swap_first = [(i, i ^ 1) for i in range(width_gx)]
    swap_second = [(i, ((i + 1) ^ 1) - 1) for i in range(1, width_gx - 1)]
    halo_first = lax.ppermute(lax.dynamic_slice_in_dim(log_conf, 2 - 2 * odd, 2, axis=1), "gx", swap_first)
    halo_second = lax.ppermute(lax.dynamic_slice_in_dim(log_conf, 2 * odd, 2, axis=1), "gx", swap_second)
    edge_cols = jnp.where(gy == 0, log_conf[:, :, ny - 2 :], log_conf[:, :, :2])
    cols = lax.ppermute(edge_cols, "gy", [(0, 1), (1, 0)]).astype(jnp.float32)

    idx = jnp.stack([odd, gy]).astype(jnp.int32)
    begun = begin(idx, log_conf, brownian, relax_rate, cols)

    near = jnp.tile(jnp.roll(kernel[..., :4], -2, axis=-1), (1, 1, 1, nz // 4))
    last = jnp.broadcast_to(kernel[..., 4:], near.shape)
    weights = jnp.stack([near, last], axis=3).reshape(comps, 5, 10, nz)
    weights = jnp.pad(weights, ((0, 0), (0, 1), (0, 6), (0, 0)))
    z = lax.broadcasted_iota(jnp.int32, (planes, nz), 1)
    k = lax.broadcasted_iota(jnp.int32, (planes, nz), 0)
    pick = jnp.concatenate([(z + 2) // 4 == k, z == 4 * k + 2] * 2, axis=1).astype(jnp.bfloat16)

    part = finish(0, idx, begun, halo_first, weights, pick, None)
    part = finish(1, idx, begun, halo_second, weights, pick, part)
    moved = lax.all_to_all(part.reshape(planes, 8, ny // 2), ("gx", "gy"), 0, 0, tiled=True)
    return pl.pallas_call(
        gather_kernel,
        out_shape=jax.ShapeDtypeStruct((comps, 1, width_gx, ny // 2), jnp.float32),
        name="gather",
    )(moved.reshape(planes * 8, ny // 2))


def solution(mesh):
    return jax.shard_map(
        local,
        mesh=mesh,
        in_specs=(
            P(None, ("grp", "gx"), "gy", None),
            P(None, ("grp", "gx"), "gy", None),
            P(("grp", "gx"), "gy", None),
            P(),
        ),
        out_specs=P(None, ("gx", "gy"), "grp", None),
        check_vma=False,
    )
```

```python
import functools

import jax
import jax.numpy as jnp
from jax import lax
from jax.experimental import pallas as pl
from jax.experimental.pallas import tpu as pltpu
from jax.sharding import PartitionSpec as P

STENCIL = 0.12 / 12.0
RELAX_STEP = 0.1
NOISE_AMP = 0.3
NC = 6
LANES = 128
LEAD = 8
TAIL = 32


def band(size):
    row = lax.broadcasted_iota(jnp.int32, (size, size), 0)
    col = lax.broadcasted_iota(jnp.int32, (size, size), 1)
    gap = jnp.abs(row - col)
    value = jnp.where(gap == 0, -30.0, jnp.where(gap == 1, 16.0, jnp.where(gap == 2, -1.0, 0.0)))
    return value.astype(jnp.bfloat16)


def position():
    return lax.rem(lax.axis_index("gx"), 2), lax.axis_index("gy")


def pack_kernel(f_ref, first_ref, second_ref, cols_ref, edges, sems):
    odd, gy = position()
    comps, rows, ny, nz = f_ref.shape
    stop = first_ref.shape[2]
    copies = []
    for c in range(comps):
        for s, (out_ref, row) in enumerate(((first_ref, 2 - 2 * odd), (second_ref, 2 * odd))):
            source = f_ref.at[c, pl.ds(row, 2), pl.ds(0, stop)]
            copies.append(pltpu.make_async_copy(source, out_ref.at[c], sems.at[2 * c + s]))
    at = pl.multiple_of((1 - gy) * (ny - 16), 16)
    copies.append(pltpu.make_async_copy(f_ref.at[:, :, pl.ds(at, 16)], edges, sems.at[2 * comps]))
    for copy in copies:
        copy.start()
    for copy in copies:
        copy.wait()
    for c in range(comps):
        for x in range(rows):
            values = edges[c, x].astype(jnp.float32)
            cols_ref[c, x] = jnp.where(gy == 0, values[14:16], values[0:2])


def pack(log_conf, stop):
    comps, rows, ny, nz = log_conf.shape
    sent = jax.ShapeDtypeStruct((comps, 2, stop, nz), log_conf.dtype)
    anywhere = pl.BlockSpec(memory_space=pl.ANY)
    return pl.pallas_call(
        pack_kernel,
        in_specs=[pl.BlockSpec(memory_space=pltpu.HBM)],
        out_specs=[anywhere, anywhere, pl.BlockSpec(memory_space=pltpu.VMEM)],
        out_shape=[sent, sent, jax.ShapeDtypeStruct((comps, rows, 2, nz), jnp.float32)],
        scratch_shapes=[
            pltpu.VMEM((comps, rows, 16, nz), log_conf.dtype),
            pltpu.SemaphoreType.DMA((2 * comps + 1,)),
        ],
        compiler_params=pltpu.CompilerParams(vmem_limit_bytes=8 * 2**20),
        name="pack",
    )(pltpu.with_memory_space_constraint(log_conf, pltpu.HBM))


def begin_kernel(f_ref, b_ref, r_ref, cols_ref, ty_ref, tz_ref, out_ref, first_ref, second_ref):
    rows, ny = f_ref.shape[1], f_ref.shape[2]
    odd, gy = position()
    step = 64
    late = first_ref.shape[2]
    first_ref[0] = f_ref[0, pl.ds(2 - 2 * odd, 2), ny - late : ny]
    second_ref[0] = f_ref[0, pl.ds(2 * odd, 2), ny - late : ny]
    for x in range(rows):
        plane = f_ref[0, x]
        for y in range(0, ny, step):
            ys = pl.ds(y, step)
            part = f_ref[0, x, ys]
            lap = jnp.dot(ty_ref[ys], plane, preferred_element_type=jnp.float32)
            lap += jnp.dot(part, tz_ref[...], preferred_element_type=jnp.float32)
            own = part.astype(jnp.float32)
            lap -= 30.0 * own
            for other in range(rows):
                if abs(other - x) == 1:
                    lap += 16.0 * f_ref[0, other, ys].astype(jnp.float32)
                elif abs(other - x) == 2:
                    lap -= f_ref[0, other, ys].astype(jnp.float32)
            rate = r_ref[x, ys].astype(jnp.float32)
            noise = b_ref[0, x, ys].astype(jnp.float32)
            out_ref[0, x, ys] = own - RELAX_STEP * rate * own + NOISE_AMP * noise + STENCIL * lap
        near_row = lax.broadcasted_iota(jnp.int32, (8, 1), 0)
        first = cols_ref[0, x, 0:1]
        second = cols_ref[0, x, 1:2]

        @pl.when(gy == 1)
        def _():
            extra = jnp.where(near_row == 0, 16.0 * second - first, jnp.where(near_row == 1, -second, 0.0))
            out_ref[0, x, 0:8] += STENCIL * extra

        @pl.when(gy == 0)
        def _():
            extra = jnp.where(near_row == 7, 16.0 * first - second, jnp.where(near_row == 6, -first, 0.0))
            out_ref[0, x, ny - 8 : ny] += STENCIL * extra


def begin(log_conf, brownian, relax_rate, cols, late):
    comps, rows, ny, nz = log_conf.shape
    whole = lambda *shape: pl.BlockSpec(shape, lambda c: (0,) * len(shape))
    block = pl.BlockSpec((1, rows, ny, nz), lambda c: (c, 0, 0, 0))
    sent = pl.BlockSpec((1, 2, late, nz), lambda c: (c, 0, 0, 0))
    return pl.pallas_call(
        begin_kernel,
        grid=(comps,),
        in_specs=[
            block,
            block,
            whole(rows, ny, nz),
            pl.BlockSpec((1, rows, 2, nz), lambda c: (c, 0, 0, 0)),
            whole(ny, ny),
            whole(nz, nz),
        ],
        out_specs=[block, sent, sent],
        out_shape=[
            jax.ShapeDtypeStruct((comps, rows, ny, nz), jnp.float32),
            jax.ShapeDtypeStruct((comps, 2, late, nz), log_conf.dtype),
            jax.ShapeDtypeStruct((comps, 2, late, nz), log_conf.dtype),
        ],
        compiler_params=pltpu.CompilerParams(vmem_limit_bytes=16 * 2**20),
        cost_estimate=pl.CostEstimate(
            flops=30 * comps * rows * ny * nz, bytes_accessed=10 * comps * rows * ny * nz, transcendentals=0
        ),
        name="begin",
    )(log_conf, brownian, relax_rate, cols, band(ny), band(nz))


def finish_kernel(start, stop, has_base, u_ref, first_ref, second_ref, w_ref, pick_ref, *refs):
    if has_base:
        base_ref, out_ref, stress, sums = refs
    else:
        out_ref, stress, sums = refs
    rows, ny, nz = u_ref.shape[1:]
    width, nj = stop - start, ny // 4
    own_j, planes, pieces = width // 4, out_ref.shape[0] // 8, nz // LANES
    odd, _ = position()
    for c in range(NC):
        for r in range(rows):
            for piece in range(pieces):
                stress[c, r, piece, 0:LEAD] = jnp.zeros((LEAD, LANES), jnp.float32)
                stress[c, r, piece, LEAD + width :] = jnp.zeros((TAIL, LANES), jnp.float32)

    for side, halo_ref in enumerate((first_ref, second_ref)):
        upper = (odd == side).astype(jnp.int32)
        near, far = 1 - upper, upper
        edge, inner = 3 * upper, 1 + upper

        def chunk(step, carry, halo_ref=halo_ref, near=near, far=far, edge=edge, inner=inner):
            y = pl.multiple_of(step * 16, 16)
            ys, us = pl.ds(y, 16), pl.ds(start + y, 16)
            updated = ([], [])
            for c in range(NC):
                close = halo_ref[c, near, ys].astype(jnp.float32)
                distant = halo_ref[c, far, ys].astype(jnp.float32)
                updated[0].append(u_ref[c, inner, us] - STENCIL * close)
                updated[1].append(u_ref[c, edge, us] + (16.0 * STENCIL) * close - STENCIL * distant)
            for row, (xx, xy, xz, yy, yz, zz) in zip((inner, edge), updated):
                xy2, xz2, yz2 = xy * xy, xz * xz, yz * yz
                values = (
                    xx + 0.5 * (xx * xx + xy2 + xz2),
                    xy + 0.5 * (xy * (xx + yy) + xz * yz),
                    xz + 0.5 * (xz * (xx + zz) + xy * yz),
                    yy + 0.5 * (xy2 + yy * yy + yz2),
                    yz + 0.5 * (yz * (yy + zz) + xy * xz),
                    zz + 0.5 * (xz2 + yz2 + zz * zz),
                )
                for c in range(NC):
                    for piece in range(pieces):
                        lanes = slice(piece * LANES, (piece + 1) * LANES)
                        stress[c, row, piece, pl.ds(y + LEAD, 16)] = values[c][:, lanes]
            return carry

        lax.fori_loop(0, width // 16, chunk, 0)

    taps = {0: ((0, 2), (1, 3), (2, 4)), 1: ((2, 0), (3, 1))}
    for c in range(NC):
        for t in range(2):
            weight = {}
            for row, a in taps[t]:
                for b in range(5):
                    for k in range(2):
                        weight[row, b, k] = w_ref[c, a, 2 * b + k : 2 * b + k + 1]
            for jb in range(own_j // 8 + 1):
                total = [None, None]
                for b in range(5 if jb < own_j // 8 else 2):
                    at = pl.ds(LEAD + 32 * jb + b - 2, 8, stride=4)
                    for row, _ in taps[t]:
                        value = jnp.concatenate([stress[c, row, piece, at] for piece in range(pieces)], axis=1)
                        for k in range(2):
                            term = value * weight[row, b, k]
                            total[k] = term if total[k] is None else total[k] + term
                for k in range(2):
                    sums[c, t, 8 * jb : 8 * jb + 8, k * nz : (k + 1) * nz] = total[k]

    def reduced(values):
        high = values.astype(jnp.bfloat16)
        low = (values - high.astype(jnp.float32)).astype(jnp.bfloat16)
        both = jnp.concatenate([high, low], axis=1)
        return lax.dot_general(
            pick_ref[...], both, (((1,), (1,)), ((), ())), preferred_element_type=jnp.float32
        )

    def put(place, value):
        at = pl.ds(place, planes, stride=8)
        if has_base:
            value = value + base_ref[at, :]
        out_ref[at, :] = value

    first_j = start // 4
    held = min(own_j + 8, nj - first_j)
    for c in range(NC):
        parts = []
        for t in range(2):
            if first_j:
                parts.append(jnp.zeros((first_j, 2 * nz), jnp.float32))
            parts.append(sums[c, t, 0:held])
            if first_j + held < nj:
                parts.append(jnp.zeros((nj - first_j - held, 2 * nz), jnp.float32))
        put(c, reduced(jnp.concatenate(parts, axis=0)))
    if stop == ny:
        beyond = [sums[c, t, own_j : own_j + 1] for c in range(NC) for t in range(2)]
        beyond.append(jnp.zeros((2 * nj - 2 * NC, 2 * nz), jnp.float32))
        put(NC, reduced(jnp.concatenate(beyond, axis=0)))
    else:
        out_ref[pl.ds(NC, planes, stride=8), :] = jnp.zeros((planes, 2 * nj), jnp.float32)
    out_ref[pl.ds(7, planes, stride=8), :] = jnp.zeros((planes, 2 * nj), jnp.float32)


def finish(start, stop, begun, halos, weights, pick, base):
    comps, rows, ny, nz = begun.shape
    planes, nj = nz // 4, ny // 4
    operands = [begun, *halos, weights, pick] + ([] if base is None else [base])
    operands = [pltpu.with_memory_space_constraint(x, pltpu.VMEM) for x in operands]
    return pl.pallas_call(
        functools.partial(finish_kernel, start, stop, base is not None),
        in_specs=[pl.BlockSpec(memory_space=pltpu.VMEM)] * len(operands),
        out_specs=pl.BlockSpec(memory_space=pltpu.VMEM),
        out_shape=jax.ShapeDtypeStruct((planes * 8, 2 * nj), jnp.float32),
        scratch_shapes=[
            pltpu.VMEM((comps, rows, nz // LANES, LEAD + stop - start + TAIL, LANES), jnp.float32),
            pltpu.VMEM((comps, 2, (stop - start) // 4 + 8, 2 * nz), jnp.float32),
        ],
        compiler_params=pltpu.CompilerParams(vmem_limit_bytes=16 * 2**20),
        cost_estimate=pl.CostEstimate(
            flops=80 * comps * (stop - start) * nz, bytes_accessed=32 * comps * (stop - start) * nz, transcendentals=0
        ),
        name="finish",
    )(*operands)


def gather_kernel(in_ref, out_ref):
    count, lanes = out_ref.shape[2], out_ref.shape[3]
    half = lanes // 2
    lane = lax.broadcasted_iota(jnp.int32, (count, lanes), 1)
    row = lax.broadcasted_iota(jnp.int32, (count, lanes), 0)
    low = lane < half
    beyond = in_ref[pl.ds(NC, count, stride=16), :]
    for c in range(NC):
        first = in_ref[pl.ds(c, count, stride=16), :]
        second = in_ref[pl.ds(8 + c, count, stride=16), :]
        own = jnp.where(low, first, pltpu.roll(second, half, 1))
        own += jnp.where(lane == half, pltpu.roll(beyond, half - 2 * c, 1), 0.0)
        after = jnp.where(low, pltpu.roll(first, half, 1), second)
        after += jnp.where(lane == half, pltpu.roll(beyond, half - 2 * c - 1, 1), 0.0)
        out_ref[c, 0] = own + jnp.where(row > 0, pltpu.roll(after, 1, 0), 0.0)


def local(log_conf, brownian, relax_rate, kernel):
    comps, rows, ny, nz = log_conf.shape
    width_gx, width_gy = lax.axis_size("gx"), lax.axis_size("gy")
    planes = nz // 4
    assert comps == NC and rows == 4 and width_gy == 2 and width_gx % 2 == 0
    assert planes == width_gx * width_gy

    swap_first = [(i, i ^ 1) for i in range(width_gx)]
    swap_second = [(i, ((i + 1) ^ 1) - 1) for i in range(1, width_gx - 1)]
    early = 3 * ny // 4
    first, second, cols = pack(log_conf, early)
    halo_early = [lax.ppermute(first, "gx", swap_first), lax.ppermute(second, "gx", swap_second)]
    cols = lax.ppermute(cols, "gy", [(0, 1), (1, 0)])
    begun, first, second = begin(log_conf, brownian, relax_rate, cols, ny - early)
    halo_late = [lax.ppermute(first, "gx", swap_first), lax.ppermute(second, "gx", swap_second)]

    near = jnp.tile(jnp.roll(kernel[..., :4], -2, axis=-1), (1, 1, 1, nz // 4))
    last = jnp.broadcast_to(kernel[..., 4:], near.shape)
    weights = jnp.stack([near, last], axis=3).reshape(comps, 5, 10, nz)
    weights = jnp.pad(weights, ((0, 0), (0, 1), (0, 6), (0, 0)))
    z = lax.broadcasted_iota(jnp.int32, (planes, nz), 1)
    k = lax.broadcasted_iota(jnp.int32, (planes, nz), 0)
    pick = jnp.concatenate([(z + 2) // 4 == k, z == 4 * k + 2] * 2, axis=1).astype(jnp.bfloat16)

    part = finish(0, early, begun, halo_early, weights, pick, None)
    part = finish(early, ny, begun, halo_late, weights, pick, part)
    moved = lax.all_to_all(part.reshape(planes, 8, ny // 2), ("gx", "gy"), 0, 0, tiled=True)
    return pl.pallas_call(
        gather_kernel,
        out_shape=jax.ShapeDtypeStruct((comps, 1, width_gx, ny // 2), jnp.float32),
        in_specs=[pl.BlockSpec(memory_space=pltpu.VMEM)],
        compiler_params=pltpu.CompilerParams(vmem_limit_bytes=4 * 2**20),
        name="gather",
    )(pltpu.with_memory_space_constraint(moved.reshape(planes * 8, ny // 2), pltpu.VMEM))


def solution(mesh):
    return jax.shard_map(
        local,
        mesh=mesh,
        in_specs=(
            P(None, ("grp", "gx"), "gy", None),
            P(None, ("grp", "gx"), "gy", None),
            P(("grp", "gx"), "gy", None),
            P(),
        ),
        out_specs=P(None, ("gx", "gy"), "grp", None),
        check_vma=False,
    )
```

```python
import functools

import jax
import jax.numpy as jnp
from jax import lax
from jax.experimental import pallas as pl
from jax.experimental.pallas import tpu as pltpu
from jax.sharding import PartitionSpec as P

STENCIL = 0.12 / 12.0
RELAX_STEP = 0.1
NOISE_AMP = 0.3
NC = 6
LANES = 128
LEAD = 8
TAIL = 32


def band(size):
    row = lax.broadcasted_iota(jnp.int32, (size, size), 0)
    col = lax.broadcasted_iota(jnp.int32, (size, size), 1)
    gap = jnp.abs(row - col)
    value = jnp.where(gap == 0, -30.0, jnp.where(gap == 1, 16.0, jnp.where(gap == 2, -1.0, 0.0)))
    return value.astype(jnp.bfloat16)


def position():
    return lax.rem(lax.axis_index("gx"), 2), lax.axis_index("gy")


def pack_kernel(second, f_ref, *refs):
    odd, gy = position()
    comps, rows, ny, nz = f_ref.shape
    if second:
        out_ref, cols_ref, sems, edges, edge_sem = refs
    else:
        out_ref, sems = refs
    row = 2 * odd if second else 2 - 2 * odd
    copies = []
    for c in range(comps):
        source = f_ref.at[c, pl.ds(row, 2), pl.ds(0, out_ref.shape[2])]
        copies.append(pltpu.make_async_copy(source, out_ref.at[c], sems.at[c]))
    if second:
        at = pl.multiple_of((1 - gy) * (ny - 16), 16)
        copies.append(pltpu.make_async_copy(f_ref.at[:, :, pl.ds(at, 16)], edges, edge_sem))
    for copy in copies:
        copy.start()
    for copy in copies:
        copy.wait()
    if second:
        for c in range(comps):
            for x in range(rows):
                values = edges[c, x].astype(jnp.float32)
                cols_ref[c, x] = jnp.where(gy == 0, values[14:16], values[0:2])


def pack(log_conf, stop, second):
    comps, rows, ny, nz = log_conf.shape
    shapes = [jax.ShapeDtypeStruct((comps, 2, stop, nz), log_conf.dtype)]
    scratch = [pltpu.SemaphoreType.DMA((comps,))]
    if second:
        shapes.append(jax.ShapeDtypeStruct((comps, rows, 2, nz), jnp.float32))
        scratch += [pltpu.VMEM((comps, rows, 16, nz), log_conf.dtype), pltpu.SemaphoreType.DMA]
    return pl.pallas_call(
        functools.partial(pack_kernel, second),
        in_specs=[pl.BlockSpec(memory_space=pltpu.HBM)],
        out_specs=[pl.BlockSpec(memory_space=pltpu.VMEM)] * len(shapes),
        out_shape=shapes,
        scratch_shapes=scratch,
        compiler_params=pltpu.CompilerParams(vmem_limit_bytes=4 * 2**20),
        name="pack",
    )(pltpu.with_memory_space_constraint(log_conf, pltpu.HBM))


def begin_kernel(
    f_ref, b_ref, r_ref, cols_ref, k_ref, out_ref, first_ref, second_ref, w_ref, pick_ref, ty_ref, tz_ref
):
    rows, ny = f_ref.shape[1], f_ref.shape[2]
    odd, gy = position()
    step = 64

    @pl.when(pl.program_id(0) == 0)
    def _():
        nz = f_ref.shape[3]
        ty_ref[...] = band(ny)
        tz_ref[...] = band(nz)
        planes = pick_ref.shape[0]
        z = lax.broadcasted_iota(jnp.int32, (planes, nz), 1)
        k = lax.broadcasted_iota(jnp.int32, (planes, nz), 0)
        for piece, chosen in enumerate((lax.shift_right_logical(z + 2, 2) == k, z == 4 * k + 2)):
            value = jnp.where(chosen, 1.0, 0.0).astype(jnp.bfloat16)
            pick_ref[:, piece * nz : (piece + 1) * nz] = value
            pick_ref[:, (piece + 2) * nz : (piece + 3) * nz] = value
        tap = (lax.broadcasted_iota(jnp.int32, (NC, nz), 1) + 2) & 3
        for a in range(5):
            for b in range(5):
                taps = k_ref[a, b]
                near = jnp.broadcast_to(taps[:, 0:1], (NC, nz))
                for e in range(1, 4):
                    near = jnp.where(tap == e, taps[:, e : e + 1], near)
                w_ref[a, b, 0] = near
                w_ref[a, b, 1] = jnp.broadcast_to(taps[:, 4:5], (NC, nz))

    late = first_ref.shape[2]
    first_ref[0] = f_ref[0, pl.ds(2 - 2 * odd, 2), ny - late : ny]
    second_ref[0] = f_ref[0, pl.ds(2 * odd, 2), ny - late : ny]
    for x in range(rows):
        plane = f_ref[0, x]
        for y in range(0, ny, step):
            ys = pl.ds(y, step)
            part = f_ref[0, x, ys]
            lap = jnp.dot(ty_ref[ys], plane, preferred_element_type=jnp.float32)
            lap += jnp.dot(part, tz_ref[...], preferred_element_type=jnp.float32)
            own = part.astype(jnp.float32)
            lap -= 30.0 * own
            for other in range(rows):
                if abs(other - x) == 1:
                    lap += 16.0 * f_ref[0, other, ys].astype(jnp.float32)
                elif abs(other - x) == 2:
                    lap -= f_ref[0, other, ys].astype(jnp.float32)
            rate = r_ref[x, ys].astype(jnp.float32)
            noise = b_ref[0, x, ys].astype(jnp.float32)
            out_ref[0, x, ys] = own - RELAX_STEP * rate * own + NOISE_AMP * noise + STENCIL * lap
        near_row = lax.broadcasted_iota(jnp.int32, (8, 1), 0)
        first = cols_ref[0, x, 0:1]
        second = cols_ref[0, x, 1:2]

        @pl.when(gy == 1)
        def _():
            extra = jnp.where(near_row == 0, 16.0 * second - first, jnp.where(near_row == 1, -second, 0.0))
            out_ref[0, x, 0:8] += STENCIL * extra

        @pl.when(gy == 0)
        def _():
            extra = jnp.where(near_row == 7, 16.0 * first - second, jnp.where(near_row == 6, -first, 0.0))
            out_ref[0, x, ny - 8 : ny] += STENCIL * extra


def begin(log_conf, brownian, relax_rate, cols, kernel, late):
    comps, rows, ny, nz = log_conf.shape
    whole = lambda *shape: pl.BlockSpec(shape, lambda c: (0,) * len(shape))
    block = pl.BlockSpec((1, rows, ny, nz), lambda c: (c, 0, 0, 0))
    sent = pl.BlockSpec((1, 2, late, nz), lambda c: (c, 0, 0, 0))
    return pl.pallas_call(
        begin_kernel,
        grid=(comps,),
        in_specs=[
            block,
            block,
            whole(rows, ny, nz),
            pl.BlockSpec((1, rows, 2, nz), lambda c: (c, 0, 0, 0)),
            whole(5, 5, comps, 5),
        ],
        out_specs=[block, sent, sent, whole(5, 5, 2, comps, nz), whole(nz // 4, 4 * nz)],
        out_shape=[
            jax.ShapeDtypeStruct((comps, rows, ny, nz), jnp.float32),
            jax.ShapeDtypeStruct((comps, 2, late, nz), log_conf.dtype),
            jax.ShapeDtypeStruct((comps, 2, late, nz), log_conf.dtype),
            jax.ShapeDtypeStruct((5, 5, 2, comps, nz), jnp.float32),
            jax.ShapeDtypeStruct((nz // 4, 4 * nz), jnp.bfloat16),
        ],
        scratch_shapes=[pltpu.VMEM((ny, ny), jnp.bfloat16), pltpu.VMEM((nz, nz), jnp.bfloat16)],
        compiler_params=pltpu.CompilerParams(vmem_limit_bytes=16 * 2**20),
        cost_estimate=pl.CostEstimate(
            flops=30 * comps * rows * ny * nz, bytes_accessed=10 * comps * rows * ny * nz, transcendentals=0
        ),
        name="begin",
    )(log_conf, brownian, relax_rate, cols, jnp.transpose(kernel, (1, 2, 0, 3)))


def finish_kernel(start, stop, has_base, u_ref, first_ref, second_ref, w_ref, pick_ref, *refs):
    if has_base:
        base_ref, out_ref, stress, sums = refs
    else:
        out_ref, stress, sums = refs
    rows, ny, nz = u_ref.shape[1:]
    width, nj = stop - start, ny // 4
    own_j, planes, pieces = width // 4, out_ref.shape[0] // 8, nz // LANES
    odd, _ = position()
    for c in range(NC):
        for r in range(rows):
            for piece in range(pieces):
                stress[c, r, piece, 0:LEAD] = jnp.zeros((LEAD, LANES), jnp.float32)
                stress[c, r, piece, LEAD + width :] = jnp.zeros((TAIL, LANES), jnp.float32)

    for side, halo_ref in enumerate((first_ref, second_ref)):
        upper = (odd == side).astype(jnp.int32)
        near, far = 1 - upper, upper
        edge, inner = 3 * upper, 1 + upper

        def chunk(step, carry, halo_ref=halo_ref, near=near, far=far, edge=edge, inner=inner):
            y = pl.multiple_of(step * 16, 16)
            ys, us = pl.ds(y, 16), pl.ds(start + y, 16)
            updated = ([], [])
            for c in range(NC):
                close = halo_ref[c, near, ys].astype(jnp.float32)
                distant = halo_ref[c, far, ys].astype(jnp.float32)
                updated[0].append(u_ref[c, inner, us] - STENCIL * close)
                updated[1].append(u_ref[c, edge, us] + (16.0 * STENCIL) * close - STENCIL * distant)
            for row, (xx, xy, xz, yy, yz, zz) in zip((inner, edge), updated):
                xy2, xz2, yz2 = xy * xy, xz * xz, yz * yz
                values = (
                    xx + 0.5 * (xx * xx + xy2 + xz2),
                    xy + 0.5 * (xy * (xx + yy) + xz * yz),
                    xz + 0.5 * (xz * (xx + zz) + xy * yz),
                    yy + 0.5 * (xy2 + yy * yy + yz2),
                    yz + 0.5 * (yz * (yy + zz) + xy * xz),
                    zz + 0.5 * (xz2 + yz2 + zz * zz),
                )
                for c in range(NC):
                    for piece in range(pieces):
                        lanes = slice(piece * LANES, (piece + 1) * LANES)
                        stress[c, row, piece, pl.ds(y + LEAD, 16)] = values[c][:, lanes]
            return carry

        lax.fori_loop(0, width // 16, chunk, 0)

    taps = {0: ((0, 2), (1, 3), (2, 4)), 1: ((2, 0), (3, 1))}
    for c in range(NC):
        for t in range(2):
            weight = {}
            for row, a in taps[t]:
                for b in range(5):
                    for k in range(2):
                        weight[row, b, k] = w_ref[a, b, k, c : c + 1]
            for jb in range(own_j // 8 + 1):
                total = [None, None]
                for b in range(5 if jb < own_j // 8 else 2):
                    at = pl.ds(LEAD + 32 * jb + b - 2, 8, stride=4)
                    for row, _ in taps[t]:
                        value = jnp.concatenate([stress[c, row, piece, at] for piece in range(pieces)], axis=1)
                        for k in range(2):
                            term = value * weight[row, b, k]
                            total[k] = term if total[k] is None else total[k] + term
                for k in range(2):
                    sums[c, t, 8 * jb : 8 * jb + 8, k * nz : (k + 1) * nz] = total[k]

    def reduced(values):
        high = values.astype(jnp.bfloat16)
        low = (values - high.astype(jnp.float32)).astype(jnp.bfloat16)
        both = jnp.concatenate([high, low], axis=1)
        return lax.dot_general(
            pick_ref[...], both, (((1,), (1,)), ((), ())), preferred_element_type=jnp.float32
        )

    def put(place, value):
        at = pl.ds(place, planes, stride=8)
        if has_base:
            value = value + base_ref[at, :]
        out_ref[at, :] = value

    first_j = start // 4
    held = min(own_j + 8, nj - first_j)
    for c in range(NC):
        parts = []
        for t in range(2):
            if first_j:
                parts.append(jnp.zeros((first_j, 2 * nz), jnp.float32))
            parts.append(sums[c, t, 0:held])
            if first_j + held < nj:
                parts.append(jnp.zeros((nj - first_j - held, 2 * nz), jnp.float32))
        put(c, reduced(jnp.concatenate(parts, axis=0)))
    if stop == ny:
        beyond = [sums[c, t, own_j : own_j + 1] for c in range(NC) for t in range(2)]
        beyond.append(jnp.zeros((2 * nj - 2 * NC, 2 * nz), jnp.float32))
        put(NC, reduced(jnp.concatenate(beyond, axis=0)))
    else:
        out_ref[pl.ds(NC, planes, stride=8), :] = jnp.zeros((planes, 2 * nj), jnp.float32)
    out_ref[pl.ds(7, planes, stride=8), :] = jnp.zeros((planes, 2 * nj), jnp.float32)


def finish(start, stop, begun, halos, weights, pick, base):
    comps, rows, ny, nz = begun.shape
    planes, nj = nz // 4, ny // 4
    operands = [begun, *halos, weights, pick] + ([] if base is None else [base])
    operands = [pltpu.with_memory_space_constraint(x, pltpu.VMEM) for x in operands]
    return pl.pallas_call(
        functools.partial(finish_kernel, start, stop, base is not None),
        in_specs=[pl.BlockSpec(memory_space=pltpu.VMEM)] * len(operands),
        out_specs=pl.BlockSpec(memory_space=pltpu.VMEM),
        out_shape=jax.ShapeDtypeStruct((planes * 8, 2 * nj), jnp.float32),
        scratch_shapes=[
            pltpu.VMEM((comps, rows, nz // LANES, LEAD + stop - start + TAIL, LANES), jnp.float32),
            pltpu.VMEM((comps, 2, (stop - start) // 4 + 8, 2 * nz), jnp.float32),
        ],
        compiler_params=pltpu.CompilerParams(vmem_limit_bytes=16 * 2**20),
        cost_estimate=pl.CostEstimate(
            flops=80 * comps * (stop - start) * nz, bytes_accessed=32 * comps * (stop - start) * nz, transcendentals=0
        ),
        name="finish",
    )(*operands)


def gather_kernel(in_ref, out_ref):
    count, lanes = out_ref.shape[2], out_ref.shape[3]
    half = lanes // 2
    lane = lax.broadcasted_iota(jnp.int32, (count, lanes), 1)
    row = lax.broadcasted_iota(jnp.int32, (count, lanes), 0)
    low = lane < half
    beyond = in_ref[pl.ds(NC, count, stride=16), :]
    for c in range(NC):
        first = in_ref[pl.ds(c, count, stride=16), :]
        second = in_ref[pl.ds(8 + c, count, stride=16), :]
        own = jnp.where(low, first, pltpu.roll(second, half, 1))
        own += jnp.where(lane == half, pltpu.roll(beyond, half - 2 * c, 1), 0.0)
        after = jnp.where(low, pltpu.roll(first, half, 1), second)
        after += jnp.where(lane == half, pltpu.roll(beyond, half - 2 * c - 1, 1), 0.0)
        out_ref[c, 0] = own + jnp.where(row > 0, pltpu.roll(after, 1, 0), 0.0)


def local(log_conf, brownian, relax_rate, kernel):
    comps, rows, ny, nz = log_conf.shape
    width_gx, width_gy = lax.axis_size("gx"), lax.axis_size("gy")
    planes = nz // 4
    assert comps == NC and rows == 4 and width_gy == 2 and width_gx % 2 == 0
    assert planes == width_gx * width_gy

    swap_first = [(i, i ^ 1) for i in range(width_gx)]
    swap_second = [(i, ((i + 1) ^ 1) - 1) for i in range(1, width_gx - 1)]
    early = 3 * ny // 4
    (first,) = pack(log_conf, early, False)
    second, cols = pack(log_conf, early, True)
    halo_early = [lax.ppermute(first, "gx", swap_first), lax.ppermute(second, "gx", swap_second)]
    cols = lax.ppermute(cols, "gy", [(0, 1), (1, 0)])
    begun, first, second, weights, pick = begin(log_conf, brownian, relax_rate, cols, kernel, ny - early)
    halo_late = [lax.ppermute(first, "gx", swap_first), lax.ppermute(second, "gx", swap_second)]

    part = finish(0, early, begun, halo_early, weights, pick, None)
    part = finish(early, ny, begun, halo_late, weights, pick, part)
    moved = lax.all_to_all(part.reshape(planes, 8, ny // 2), ("gx", "gy"), 0, 0, tiled=True)
    return pl.pallas_call(
        gather_kernel,
        out_shape=jax.ShapeDtypeStruct((comps, 1, width_gx, ny // 2), jnp.float32),
        in_specs=[pl.BlockSpec(memory_space=pltpu.VMEM)],
        compiler_params=pltpu.CompilerParams(vmem_limit_bytes=4 * 2**20),
        name="gather",
    )(pltpu.with_memory_space_constraint(moved.reshape(planes * 8, ny // 2), pltpu.VMEM))


def solution(mesh):
    return jax.shard_map(
        local,
        mesh=mesh,
        in_specs=(
            P(None, ("grp", "gx"), "gy", None),
            P(None, ("grp", "gx"), "gy", None),
            P(("grp", "gx"), "gy", None),
            P(),
        ),
        out_specs=P(None, ("gx", "gy"), "grp", None),
        check_vma=False,
    )
```

```python
import functools

import jax
import jax.numpy as jnp
from jax import lax
from jax.experimental import pallas as pl
from jax.experimental.pallas import tpu as pltpu
from jax.sharding import PartitionSpec as P

STENCIL = 0.12 / 12.0
RELAX_STEP = 0.1
NOISE_AMP = 0.3
NC = 6
LANES = 128
LEAD = 8
TAIL = 32


def band(size):
    row = lax.broadcasted_iota(jnp.int32, (size, size), 0)
    col = lax.broadcasted_iota(jnp.int32, (size, size), 1)
    gap = jnp.abs(row - col)
    value = jnp.where(gap == 0, -30.0, jnp.where(gap == 1, 16.0, jnp.where(gap == 2, -1.0, 0.0)))
    return value.astype(jnp.bfloat16)


def position():
    return lax.rem(lax.axis_index("gx"), 2), lax.axis_index("gy")


def pack_kernel(second, f_ref, *refs):
    odd, gy = position()
    comps, rows, ny, nz = f_ref.shape
    if second:
        out_ref, cols_ref, sems, edges, edge_sem = refs
    else:
        out_ref, sems = refs
    row = 2 * odd if second else 2 - 2 * odd
    copies = []
    for c in range(comps):
        source = f_ref.at[c, pl.ds(row, 2), pl.ds(0, out_ref.shape[2])]
        copies.append(pltpu.make_async_copy(source, out_ref.at[c], sems.at[c]))
    if second:
        at = pl.multiple_of((1 - gy) * (ny - 16), 16)
        copies.append(pltpu.make_async_copy(f_ref.at[:, :, pl.ds(at, 16)], edges, edge_sem))
    for copy in copies:
        copy.start()
    for copy in copies:
        copy.wait()
    if second:
        for c in range(comps):
            for x in range(rows):
                values = edges[c, x].astype(jnp.float32)
                cols_ref[c, x] = jnp.where(gy == 0, values[14:16], values[0:2])


def pack(log_conf, stop, second):
    comps, rows, ny, nz = log_conf.shape
    shapes = [jax.ShapeDtypeStruct((comps, 2, stop, nz), log_conf.dtype)]
    scratch = [pltpu.SemaphoreType.DMA((comps,))]
    if second:
        shapes.append(jax.ShapeDtypeStruct((comps, rows, 2, nz), jnp.float32))
        scratch += [pltpu.VMEM((comps, rows, 16, nz), log_conf.dtype), pltpu.SemaphoreType.DMA]
    return pl.pallas_call(
        functools.partial(pack_kernel, second),
        in_specs=[pl.BlockSpec(memory_space=pltpu.HBM)],
        out_specs=[pl.BlockSpec(memory_space=pltpu.VMEM)] * len(shapes),
        out_shape=shapes,
        scratch_shapes=scratch,
        compiler_params=pltpu.CompilerParams(vmem_limit_bytes=4 * 2**20),
        name="pack",
    )(pltpu.with_memory_space_constraint(log_conf, pltpu.HBM))


def begin_kernel(
    cuts, f_ref, b_ref, r_ref, cols_ref, k_ref, out_ref, w_ref, pick_ref, *refs
):
    rows, ny = f_ref.shape[1], f_ref.shape[2]
    odd, gy = position()
    ty_ref, tz_ref = refs[-2:]
    step = 64

    @pl.when(pl.program_id(0) == 0)
    def _():
        nz = f_ref.shape[3]
        ty_ref[...] = band(ny)
        tz_ref[...] = band(nz)
        planes = pick_ref.shape[0]
        z = lax.broadcasted_iota(jnp.int32, (planes, nz), 1)
        k = lax.broadcasted_iota(jnp.int32, (planes, nz), 0)
        for piece, chosen in enumerate((lax.shift_right_logical(z + 2, 2) == k, z == 4 * k + 2)):
            value = jnp.where(chosen, 1.0, 0.0).astype(jnp.bfloat16)
            pick_ref[:, piece * nz : (piece + 1) * nz] = value
            pick_ref[:, (piece + 2) * nz : (piece + 3) * nz] = value
        tap = (lax.broadcasted_iota(jnp.int32, (NC, nz), 1) + 2) & 3
        for a in range(5):
            for b in range(5):
                taps = k_ref[a, b]
                near = jnp.broadcast_to(taps[:, 0:1], (NC, nz))
                for e in range(1, 4):
                    near = jnp.where(tap == e, taps[:, e : e + 1], near)
                w_ref[a, b, 0] = near
                w_ref[a, b, 1] = jnp.broadcast_to(taps[:, 4:5], (NC, nz))

    for (start, stop), first_ref, second_ref in zip(cuts, refs[0:-2:2], refs[1:-2:2]):
        first_ref[0] = f_ref[0, pl.ds(2 - 2 * odd, 2), start:stop]
        second_ref[0] = f_ref[0, pl.ds(2 * odd, 2), start:stop]
    for x in range(rows):
        plane = f_ref[0, x]
        for y in range(0, ny, step):
            ys = pl.ds(y, step)
            part = f_ref[0, x, ys]
            lap = jnp.dot(ty_ref[ys], plane, preferred_element_type=jnp.float32)
            lap += jnp.dot(part, tz_ref[...], preferred_element_type=jnp.float32)
            own = part.astype(jnp.float32)
            lap -= 30.0 * own
            for other in range(rows):
                if abs(other - x) == 1:
                    lap += 16.0 * f_ref[0, other, ys].astype(jnp.float32)
                elif abs(other - x) == 2:
                    lap -= f_ref[0, other, ys].astype(jnp.float32)
            rate = r_ref[x, ys].astype(jnp.float32)
            noise = b_ref[0, x, ys].astype(jnp.float32)
            out_ref[0, x, ys] = own - RELAX_STEP * rate * own + NOISE_AMP * noise + STENCIL * lap
        near_row = lax.broadcasted_iota(jnp.int32, (8, 1), 0)
        first = cols_ref[0, x, 0:1]
        second = cols_ref[0, x, 1:2]

        @pl.when(gy == 1)
        def _():
            extra = jnp.where(near_row == 0, 16.0 * second - first, jnp.where(near_row == 1, -second, 0.0))
            out_ref[0, x, 0:8] += STENCIL * extra

        @pl.when(gy == 0)
        def _():
            extra = jnp.where(near_row == 7, 16.0 * first - second, jnp.where(near_row == 6, -first, 0.0))
            out_ref[0, x, ny - 8 : ny] += STENCIL * extra


def begin(log_conf, brownian, relax_rate, cols, kernel, cuts):
    comps, rows, ny, nz = log_conf.shape
    whole = lambda *shape: pl.BlockSpec(shape, lambda c: (0,) * len(shape))
    block = pl.BlockSpec((1, rows, ny, nz), lambda c: (c, 0, 0, 0))
    heights = [stop - start for start, stop in cuts for _ in range(2)]
    return pl.pallas_call(
        functools.partial(begin_kernel, cuts),
        grid=(comps,),
        in_specs=[
            block,
            block,
            whole(rows, ny, nz),
            pl.BlockSpec((1, rows, 2, nz), lambda c: (c, 0, 0, 0)),
            whole(5, 5, comps, 5),
        ],
        out_specs=[block, whole(5, 5, 2, comps, nz), whole(nz // 4, 4 * nz)]
        + [pl.BlockSpec((1, 2, height, nz), lambda c: (c, 0, 0, 0)) for height in heights],
        out_shape=[
            jax.ShapeDtypeStruct((comps, rows, ny, nz), jnp.float32),
            jax.ShapeDtypeStruct((5, 5, 2, comps, nz), jnp.float32),
            jax.ShapeDtypeStruct((nz // 4, 4 * nz), jnp.bfloat16),
        ]
        + [jax.ShapeDtypeStruct((comps, 2, height, nz), log_conf.dtype) for height in heights],
        scratch_shapes=[pltpu.VMEM((ny, ny), jnp.bfloat16), pltpu.VMEM((nz, nz), jnp.bfloat16)],
        compiler_params=pltpu.CompilerParams(vmem_limit_bytes=16 * 2**20),
        cost_estimate=pl.CostEstimate(
            flops=30 * comps * rows * ny * nz, bytes_accessed=10 * comps * rows * ny * nz, transcendentals=0
        ),
        name="begin",
    )(*(pltpu.with_memory_space_constraint(x, pltpu.HBM) for x in (log_conf, brownian, relax_rate)), cols, jnp.transpose(kernel, (1, 2, 0, 3)))


def finish_kernel(start, stop, has_base, u_ref, first_ref, second_ref, w_ref, pick_ref, *refs):
    if has_base:
        base_ref, out_ref, stress, sums = refs
    else:
        out_ref, stress, sums = refs
    rows, ny, nz = u_ref.shape[1:]
    width, nj = stop - start, ny // 4
    own_j, planes, pieces = width // 4, out_ref.shape[0] // 8, nz // LANES
    odd, _ = position()
    compact = len(sums.shape) == 2
    if compact:
        for t in range(2):
            sums[t * nj + 8 * NC : (t + 1) * nj] = jnp.zeros((nj - 8 * NC, 2 * nz), jnp.float32)
    for c in range(NC):
        for r in range(rows):
            for piece in range(pieces):
                stress[c, r, piece, 0:LEAD] = jnp.zeros((LEAD, LANES), jnp.float32)
                stress[c, r, piece, LEAD + width :] = jnp.zeros((TAIL, LANES), jnp.float32)

    for side, halo_ref in enumerate((first_ref, second_ref)):
        upper = (odd == side).astype(jnp.int32)
        near, far = 1 - upper, upper
        edge, inner = 3 * upper, 1 + upper

        def chunk(step, carry, halo_ref=halo_ref, near=near, far=far, edge=edge, inner=inner):
            y = pl.multiple_of(step * 16, 16)
            ys, us = pl.ds(y, 16), pl.ds(start + y, 16)
            updated = ([], [])
            for c in range(NC):
                close = halo_ref[c, near, ys].astype(jnp.float32)
                distant = halo_ref[c, far, ys].astype(jnp.float32)
                updated[0].append(u_ref[c, inner, us] - STENCIL * close)
                updated[1].append(u_ref[c, edge, us] + (16.0 * STENCIL) * close - STENCIL * distant)
            for row, (xx, xy, xz, yy, yz, zz) in zip((inner, edge), updated):
                xy2, xz2, yz2 = xy * xy, xz * xz, yz * yz
                values = (
                    xx + 0.5 * (xx * xx + xy2 + xz2),
                    xy + 0.5 * (xy * (xx + yy) + xz * yz),
                    xz + 0.5 * (xz * (xx + zz) + xy * yz),
                    yy + 0.5 * (xy2 + yy * yy + yz2),
                    yz + 0.5 * (yz * (yy + zz) + xy * xz),
                    zz + 0.5 * (xz2 + yz2 + zz * zz),
                )
                for c in range(NC):
                    for piece in range(pieces):
                        lanes = slice(piece * LANES, (piece + 1) * LANES)
                        stress[c, row, piece, pl.ds(y + LEAD, 16)] = values[c][:, lanes]
            return carry

        lax.fori_loop(0, width // 16, chunk, 0)

    taps = {0: ((0, 2), (1, 3), (2, 4)), 1: ((2, 0), (3, 1))}
    for c in range(NC):
        for t in range(2):
            weight = {}
            for row, a in taps[t]:
                for b in range(5):
                    for k in range(2):
                        weight[row, b, k] = w_ref[a, b, k, c : c + 1]
            for jb in range(own_j // 8 + 1):
                total = [None, None]
                for b in range(5 if jb < own_j // 8 else 2):
                    at = pl.ds(LEAD + 32 * jb + b - 2, 8, stride=4)
                    for row, _ in taps[t]:
                        value = jnp.concatenate([stress[c, row, piece, at] for piece in range(pieces)], axis=1)
                        for k in range(2):
                            term = value * weight[row, b, k]
                            total[k] = term if total[k] is None else total[k] + term
                for k in range(2):
                    lanes = slice(k * nz, (k + 1) * nz)
                    if not compact:
                        sums[c, t, 8 * jb : 8 * jb + 8, lanes] = total[k]
                    elif jb == 0:
                        sums[t * nj + 8 * c : t * nj + 8 * c + 8, lanes] = total[k]
                    else:
                        at = t * nj + 8 * NC + c
                        sums[at : at + 1, lanes] = total[k][0:1]

    def reduced(values):
        high = values.astype(jnp.bfloat16)
        low = (values - high.astype(jnp.float32)).astype(jnp.bfloat16)
        both = jnp.concatenate([high, low], axis=1)
        return lax.dot_general(
            pick_ref[...], both, (((1,), (1,)), ((), ())), preferred_element_type=jnp.float32
        )

    def put(place, value):
        at = pl.ds(place, planes, stride=8)
        if has_base:
            value = value + base_ref[at, :]
        out_ref[at, :] = value

    if compact:
        lane = lax.broadcasted_iota(jnp.int32, (planes, 2 * nj), 1)
        spread = reduced(sums[...])
        for c in range(NC):
            moved = pltpu.roll(spread, nj - 8 - 8 * c, 1)
            put(c, jnp.where((lane & (nj - 1)) >= nj - 8, moved, 0.0))
        out_ref[pl.ds(NC, planes, stride=8), :] = spread
        out_ref[pl.ds(7, planes, stride=8), :] = jnp.zeros((planes, 2 * nj), jnp.float32)
        return

    first_j = start // 4
    held = min(own_j + 8, nj - first_j)
    for c in range(NC):
        parts = []
        for t in range(2):
            if first_j:
                parts.append(jnp.zeros((first_j, 2 * nz), jnp.float32))
            parts.append(sums[c, t, 0:held])
            if first_j + held < nj:
                parts.append(jnp.zeros((nj - first_j - held, 2 * nz), jnp.float32))
        put(c, reduced(jnp.concatenate(parts, axis=0)))
    for place in (NC, 7):
        out_ref[pl.ds(place, planes, stride=8), :] = jnp.zeros((planes, 2 * nj), jnp.float32)


def finish(start, stop, begun, halos, weights, pick, base):
    comps, rows, ny, nz = begun.shape
    planes, nj = nz // 4, ny // 4
    places = (2 * nj, 2 * nz) if stop == ny else (comps, 2, (stop - start) // 4 + 8, 2 * nz)
    operands = [begun, *halos, weights, pick] + ([] if base is None else [base])
    operands = [pltpu.with_memory_space_constraint(x, pltpu.VMEM) for x in operands]
    return pl.pallas_call(
        functools.partial(finish_kernel, start, stop, base is not None),
        in_specs=[pl.BlockSpec(memory_space=pltpu.VMEM)] * len(operands),
        out_specs=pl.BlockSpec(memory_space=pltpu.VMEM),
        out_shape=jax.ShapeDtypeStruct((planes * 8, 2 * nj), jnp.float32),
        scratch_shapes=[
            pltpu.VMEM((comps, rows, nz // LANES, LEAD + stop - start + TAIL, LANES), jnp.float32),
            pltpu.VMEM(places, jnp.float32),
        ],
        compiler_params=pltpu.CompilerParams(vmem_limit_bytes=16 * 2**20),
        cost_estimate=pl.CostEstimate(
            flops=80 * comps * (stop - start) * nz, bytes_accessed=32 * comps * (stop - start) * nz, transcendentals=0
        ),
        name="finish",
    )(*operands)


def gather_kernel(in_ref, out_ref):
    count, lanes = out_ref.shape[2], out_ref.shape[3]
    half = lanes // 2
    lane = lax.broadcasted_iota(jnp.int32, (count, lanes), 1)
    row = lax.broadcasted_iota(jnp.int32, (count, lanes), 0)
    low = lane < half
    beyond = in_ref[pl.ds(NC, count, stride=16), :]
    for c in range(NC):
        first = in_ref[pl.ds(c, count, stride=16), :]
        second = in_ref[pl.ds(8 + c, count, stride=16), :]
        own = jnp.where(low, first, pltpu.roll(second, half, 1))
        own += jnp.where(lane == half, pltpu.roll(beyond, half - 8 * NC - c, 1), 0.0)
        after = jnp.where(low, pltpu.roll(first, half, 1), second)
        after += jnp.where(lane == half, pltpu.roll(beyond, lanes - 8 * NC - c, 1), 0.0)
        out_ref[c, 0] = own + jnp.where(row > 0, pltpu.roll(after, 1, 0), 0.0)


def local(log_conf, brownian, relax_rate, kernel):
    comps, rows, ny, nz = log_conf.shape
    width_gx, width_gy = lax.axis_size("gx"), lax.axis_size("gy")
    planes = nz // 4
    assert comps == NC and rows == 4 and width_gy == 2 and width_gx % 2 == 0
    assert planes == width_gx * width_gy and ny == 256

    swap_first = [(i, i ^ 1) for i in range(width_gx)]
    swap_second = [(i, ((i + 1) ^ 1) - 1) for i in range(1, width_gx - 1)]
    cuts = [(0, ny // 2), (ny // 2, 7 * ny // 8), (7 * ny // 8, ny)]
    early = cuts[0][1]
    (first,) = pack(log_conf, early, False)
    second, cols = pack(log_conf, early, True)
    halos = [[lax.ppermute(first, "gx", swap_first), lax.ppermute(second, "gx", swap_second)]]
    cols = lax.ppermute(cols, "gy", [(0, 1), (1, 0)])
    begun, weights, pick, *sent = begin(log_conf, brownian, relax_rate, cols, kernel, cuts[1:])
    for first, second in zip(sent[0::2], sent[1::2]):
        halos.append([lax.ppermute(first, "gx", swap_first), lax.ppermute(second, "gx", swap_second)])

    part = None
    for (start, stop), pair in zip(cuts, halos):
        part = finish(start, stop, begun, pair, weights, pick, part)
    moved = lax.all_to_all(part.reshape(planes, 8, ny // 2), ("gx", "gy"), 0, 0, tiled=True)
    return pl.pallas_call(
        gather_kernel,
        out_shape=jax.ShapeDtypeStruct((comps, 1, width_gx, ny // 2), jnp.float32),
        in_specs=[pl.BlockSpec(memory_space=pltpu.VMEM)],
        compiler_params=pltpu.CompilerParams(vmem_limit_bytes=4 * 2**20),
        name="gather",
    )(pltpu.with_memory_space_constraint(moved.reshape(planes * 8, ny // 2), pltpu.VMEM))


def solution(mesh):
    return jax.shard_map(
        local,
        mesh=mesh,
        in_specs=(
            P(None, ("grp", "gx"), "gy", None),
            P(None, ("grp", "gx"), "gy", None),
            P(("grp", "gx"), "gy", None),
            P(),
        ),
        out_specs=P(None, ("gx", "gy"), "grp", None),
        check_vma=False,
    )
```

```python
import functools

import jax
import jax.numpy as jnp
from jax import lax
from jax.experimental import pallas as pl
from jax.experimental.pallas import tpu as pltpu
from jax.sharding import PartitionSpec as P

STENCIL = 0.12 / 12.0
RELAX_STEP = 0.1
NOISE_AMP = 0.3
NC = 6
LANES = 128
ROWS = NC + 1
LEAD = 8
TAIL = 32


def band(size):
    row = lax.broadcasted_iota(jnp.int32, (size, size), 0)
    col = lax.broadcasted_iota(jnp.int32, (size, size), 1)
    gap = jnp.abs(row - col)
    value = jnp.where(gap == 0, -30.0, jnp.where(gap == 1, 16.0, jnp.where(gap == 2, -1.0, 0.0)))
    return value.astype(jnp.bfloat16)


def position():
    return lax.rem(lax.axis_index("gx"), 2), lax.axis_index("gy")


def pack_kernel(second, f_ref, *refs):
    odd, gy = position()
    comps, rows, ny, nz = f_ref.shape
    if second:
        out_ref, cols_ref, sems, edges, edge_sem = refs
    else:
        out_ref, sems = refs
    row = 2 * odd if second else 2 - 2 * odd
    copies = []
    copies.append(pltpu.make_async_copy(f_ref.at[:, pl.ds(row, 2), pl.ds(0, out_ref.shape[2])], out_ref, sems))
    if second:
        at = pl.multiple_of((1 - gy) * (ny - 16), 16)
        copies.append(pltpu.make_async_copy(f_ref.at[:, :, pl.ds(at, 16)], edges, edge_sem))
    for copy in copies:
        copy.start()
    for copy in copies:
        copy.wait()
    if second:
        for c in range(comps):
            for x in range(rows):
                values = edges[c, x].astype(jnp.float32)
                cols_ref[c, x] = jnp.where(gy == 0, values[14:16], values[0:2])


def pack(log_conf, stop, second):
    comps, rows, ny, nz = log_conf.shape
    shapes = [jax.ShapeDtypeStruct((comps, 2, stop, nz), log_conf.dtype)]
    scratch = [pltpu.SemaphoreType.DMA]
    if second:
        shapes.append(jax.ShapeDtypeStruct((comps, rows, 2, nz), jnp.float32))
        scratch += [pltpu.VMEM((comps, rows, 16, nz), log_conf.dtype), pltpu.SemaphoreType.DMA]
    return pl.pallas_call(
        functools.partial(pack_kernel, second),
        in_specs=[pl.BlockSpec(memory_space=pltpu.HBM)],
        out_specs=[pl.BlockSpec(memory_space=pltpu.VMEM)] * len(shapes),
        out_shape=shapes,
        scratch_shapes=scratch,
        compiler_params=pltpu.CompilerParams(vmem_limit_bytes=4 * 2**20),
        name="pack",
    )(pltpu.with_memory_space_constraint(log_conf, pltpu.HBM))


def begin_kernel(
    cuts, f_ref, b_ref, r_ref, cols_ref, k_ref, out_ref, w_ref, pick_ref, *refs
):
    rows, ny = f_ref.shape[1], f_ref.shape[2]
    odd, gy = position()
    ty_ref, tz_ref = refs[-2:]
    step = 64

    @pl.when(pl.program_id(0) == 0)
    def _():
        nz = f_ref.shape[3]
        ty_ref[...] = band(ny)
        tz_ref[...] = band(nz)
        planes = pick_ref.shape[0]
        z = lax.broadcasted_iota(jnp.int32, (planes, nz), 1)
        k = lax.broadcasted_iota(jnp.int32, (planes, nz), 0)
        for piece, chosen in enumerate((lax.shift_right_logical(z + 2, 2) == k, z == 4 * k + 2)):
            value = jnp.where(chosen, 1.0, 0.0).astype(jnp.bfloat16)
            pick_ref[:, piece * nz : (piece + 1) * nz] = value
            pick_ref[:, (piece + 2) * nz : (piece + 3) * nz] = value
        tap = (lax.broadcasted_iota(jnp.int32, (NC, nz), 1) + 2) & 3
        for a in range(5):
            for b in range(5):
                taps = k_ref[a, b]
                near = jnp.broadcast_to(taps[:, 0:1], (NC, nz))
                for e in range(1, 4):
                    near = jnp.where(tap == e, taps[:, e : e + 1], near)
                w_ref[a, b, 0] = near
                w_ref[a, b, 1] = jnp.broadcast_to(taps[:, 4:5], (NC, nz))

    for (start, stop), first_ref, second_ref in zip(cuts, refs[0:-2:2], refs[1:-2:2]):
        first_ref[0] = f_ref[0, pl.ds(2 - 2 * odd, 2), start:stop]
        second_ref[0] = f_ref[0, pl.ds(2 * odd, 2), start:stop]
    for x in range(rows):
        plane = f_ref[0, x]
        for y in range(0, ny, step):
            ys = pl.ds(y, step)
            part = f_ref[0, x, ys]
            lap = jnp.dot(ty_ref[ys], plane, preferred_element_type=jnp.float32)
            lap += jnp.dot(part, tz_ref[...], preferred_element_type=jnp.float32)
            own = part.astype(jnp.float32)
            lap -= 30.0 * own
            for other in range(rows):
                if abs(other - x) == 1:
                    lap += 16.0 * f_ref[0, other, ys].astype(jnp.float32)
                elif abs(other - x) == 2:
                    lap -= f_ref[0, other, ys].astype(jnp.float32)
            rate = r_ref[x, ys].astype(jnp.float32)
            noise = b_ref[0, x, ys].astype(jnp.float32)
            out_ref[0, x, ys] = own - RELAX_STEP * rate * own + NOISE_AMP * noise + STENCIL * lap
        near_row = lax.broadcasted_iota(jnp.int32, (8, 1), 0)
        first = cols_ref[0, x, 0:1]
        second = cols_ref[0, x, 1:2]

        @pl.when(gy == 1)
        def _():
            extra = jnp.where(near_row == 0, 16.0 * second - first, jnp.where(near_row == 1, -second, 0.0))
            out_ref[0, x, 0:8] += STENCIL * extra

        @pl.when(gy == 0)
        def _():
            extra = jnp.where(near_row == 7, 16.0 * first - second, jnp.where(near_row == 6, -first, 0.0))
            out_ref[0, x, ny - 8 : ny] += STENCIL * extra


def begin(log_conf, brownian, relax_rate, cols, kernel, cuts):
    comps, rows, ny, nz = log_conf.shape
    whole = lambda *shape: pl.BlockSpec(shape, lambda c: (0,) * len(shape))
    block = pl.BlockSpec((1, rows, ny, nz), lambda c: (c, 0, 0, 0))
    heights = [stop - start for start, stop in cuts for _ in range(2)]
    return pl.pallas_call(
        functools.partial(begin_kernel, cuts),
        grid=(comps,),
        in_specs=[
            block,
            block,
            whole(rows, ny, nz),
            pl.BlockSpec((1, rows, 2, nz), lambda c: (c, 0, 0, 0)),
            whole(5, 5, comps, 5),
        ],
        out_specs=[block, whole(5, 5, 2, comps, nz), whole(nz // 4, 4 * nz)]
        + [pl.BlockSpec((1, 2, height, nz), lambda c: (c, 0, 0, 0)) for height in heights],
        out_shape=[
            jax.ShapeDtypeStruct((comps, rows, ny, nz), jnp.float32),
            jax.ShapeDtypeStruct((5, 5, 2, comps, nz), jnp.float32),
            jax.ShapeDtypeStruct((nz // 4, 4 * nz), jnp.bfloat16),
        ]
        + [jax.ShapeDtypeStruct((comps, 2, height, nz), log_conf.dtype) for height in heights],
        scratch_shapes=[pltpu.VMEM((ny, ny), jnp.bfloat16), pltpu.VMEM((nz, nz), jnp.bfloat16)],
        compiler_params=pltpu.CompilerParams(vmem_limit_bytes=16 * 2**20),
        cost_estimate=pl.CostEstimate(
            flops=30 * comps * rows * ny * nz, bytes_accessed=10 * comps * rows * ny * nz, transcendentals=0
        ),
        name="begin",
    )(*(pltpu.with_memory_space_constraint(x, pltpu.HBM) for x in (log_conf, brownian, relax_rate)), cols, jnp.transpose(kernel, (1, 2, 0, 3)))


def finish_kernel(start, stop, has_base, u_ref, first_ref, second_ref, w_ref, pick_ref, *refs):
    if has_base:
        base_ref, out_ref, stress, sums = refs
    else:
        out_ref, stress, sums = refs
    rows, ny, nz = u_ref.shape[1:]
    width, nj = stop - start, ny // 4
    own_j, planes, pieces = width // 4, out_ref.shape[0] // ROWS, nz // LANES
    odd, _ = position()
    compact = len(sums.shape) == 2
    if compact:
        for t in range(2):
            sums[t * nj + 8 * NC : (t + 1) * nj] = jnp.zeros((nj - 8 * NC, 2 * nz), jnp.float32)
    for c in range(NC):
        for r in range(rows):
            for piece in range(pieces):
                stress[c, r, piece, 0:LEAD] = jnp.zeros((LEAD, LANES), jnp.float32)
                stress[c, r, piece, LEAD + width :] = jnp.zeros((TAIL, LANES), jnp.float32)

    for side, halo_ref in enumerate((first_ref, second_ref)):
        upper = (odd == side).astype(jnp.int32)
        near, far = 1 - upper, upper
        edge, inner = 3 * upper, 1 + upper

        def chunk(step, carry, halo_ref=halo_ref, near=near, far=far, edge=edge, inner=inner):
            y = pl.multiple_of(step * 16, 16)
            ys, us = pl.ds(y, 16), pl.ds(start + y, 16)
            updated = ([], [])
            for c in range(NC):
                close = halo_ref[c, near, ys].astype(jnp.float32)
                distant = halo_ref[c, far, ys].astype(jnp.float32)
                updated[0].append(u_ref[c, inner, us] - STENCIL * close)
                updated[1].append(u_ref[c, edge, us] + (16.0 * STENCIL) * close - STENCIL * distant)
            for row, (xx, xy, xz, yy, yz, zz) in zip((inner, edge), updated):
                xy2, xz2, yz2 = xy * xy, xz * xz, yz * yz
                values = (
                    xx + 0.5 * (xx * xx + xy2 + xz2),
                    xy + 0.5 * (xy * (xx + yy) + xz * yz),
                    xz + 0.5 * (xz * (xx + zz) + xy * yz),
                    yy + 0.5 * (xy2 + yy * yy + yz2),
                    yz + 0.5 * (yz * (yy + zz) + xy * xz),
                    zz + 0.5 * (xz2 + yz2 + zz * zz),
                )
                for c in range(NC):
                    for piece in range(pieces):
                        lanes = slice(piece * LANES, (piece + 1) * LANES)
                        stress[c, row, piece, pl.ds(y + LEAD, 16)] = values[c][:, lanes]
            return carry

        lax.fori_loop(0, width // 16, chunk, 0)

    taps = {0: ((0, 2), (1, 3), (2, 4)), 1: ((2, 0), (3, 1))}
    for c in range(NC):
        for t in range(2):
            weight = {}
            for row, a in taps[t]:
                for b in range(5):
                    for k in range(2):
                        weight[row, b, k] = w_ref[a, b, k, c : c + 1]
            for jb in range(own_j // 8 + 1):
                total = [None, None]
                for b in range(5 if jb < own_j // 8 else 2):
                    at = pl.ds(LEAD + 32 * jb + b - 2, 8, stride=4)
                    for row, _ in taps[t]:
                        value = jnp.concatenate([stress[c, row, piece, at] for piece in range(pieces)], axis=1)
                        for k in range(2):
                            term = value * weight[row, b, k]
                            total[k] = term if total[k] is None else total[k] + term
                for k in range(2):
                    lanes = slice(k * nz, (k + 1) * nz)
                    if not compact:
                        sums[c, t, 8 * jb : 8 * jb + 8, lanes] = total[k]
                    elif jb == 0:
                        sums[t * nj + 8 * c : t * nj + 8 * c + 8, lanes] = total[k]
                    else:
                        at = t * nj + 8 * NC + c
                        sums[at : at + 1, lanes] = total[k][0:1]

    def reduced(values):
        high = values.astype(jnp.bfloat16)
        low = (values - high.astype(jnp.float32)).astype(jnp.bfloat16)
        both = jnp.concatenate([high, low], axis=1)
        return lax.dot_general(
            pick_ref[...], both, (((1,), (1,)), ((), ())), preferred_element_type=jnp.float32
        )

    def put(place, value):
        at = pl.ds(place, planes, stride=ROWS)
        if has_base:
            value = value + base_ref[at, :]
        out_ref[at, :] = value

    if compact:
        lane = lax.broadcasted_iota(jnp.int32, (planes, 2 * nj), 1)
        spread = reduced(sums[...])
        for c in range(NC):
            moved = pltpu.roll(spread, nj - 8 - 8 * c, 1)
            put(c, jnp.where((lane & (nj - 1)) >= nj - 8, moved, 0.0))
        out_ref[pl.ds(NC, planes, stride=ROWS), :] = spread
        return

    first_j = start // 4
    held = min(own_j + 8, nj - first_j)
    for c in range(NC):
        parts = []
        for t in range(2):
            if first_j:
                parts.append(jnp.zeros((first_j, 2 * nz), jnp.float32))
            parts.append(sums[c, t, 0:held])
            if first_j + held < nj:
                parts.append(jnp.zeros((nj - first_j - held, 2 * nz), jnp.float32))
        put(c, reduced(jnp.concatenate(parts, axis=0)))
    out_ref[pl.ds(NC, planes, stride=ROWS), :] = jnp.zeros((planes, 2 * nj), jnp.float32)


def finish(start, stop, begun, halos, weights, pick, base):
    comps, rows, ny, nz = begun.shape
    planes, nj = nz // 4, ny // 4
    places = (2 * nj, 2 * nz) if stop == ny else (comps, 2, (stop - start) // 4 + 8, 2 * nz)
    operands = [begun, *halos, weights, pick] + ([] if base is None else [base])
    operands = [pltpu.with_memory_space_constraint(x, pltpu.VMEM) for x in operands]
    return pl.pallas_call(
        functools.partial(finish_kernel, start, stop, base is not None),
        in_specs=[pl.BlockSpec(memory_space=pltpu.VMEM)] * len(operands),
        out_specs=pl.BlockSpec(memory_space=pltpu.VMEM),
        out_shape=jax.ShapeDtypeStruct((planes * ROWS, 2 * nj), jnp.float32),
        scratch_shapes=[
            pltpu.VMEM((comps, rows, nz // LANES, LEAD + stop - start + TAIL, LANES), jnp.float32),
            pltpu.VMEM(places, jnp.float32),
        ],
        compiler_params=pltpu.CompilerParams(vmem_limit_bytes=16 * 2**20),
        cost_estimate=pl.CostEstimate(
            flops=80 * comps * (stop - start) * nz, bytes_accessed=32 * comps * (stop - start) * nz, transcendentals=0
        ),
        name="finish",
    )(*operands)


def gather_kernel(in_ref, out_ref):
    count, lanes = out_ref.shape[2], out_ref.shape[3]
    half = lanes // 2
    lane = lax.broadcasted_iota(jnp.int32, (count, lanes), 1)
    row = lax.broadcasted_iota(jnp.int32, (count, lanes), 0)
    low = lane < half
    beyond = in_ref[pl.ds(NC, count, stride=2 * ROWS), :]
    for c in range(NC):
        first = in_ref[pl.ds(c, count, stride=2 * ROWS), :]
        second = in_ref[pl.ds(ROWS + c, count, stride=2 * ROWS), :]
        own = jnp.where(low, first, pltpu.roll(second, half, 1))
        own += jnp.where(lane == half, pltpu.roll(beyond, half - 8 * NC - c, 1), 0.0)
        after = jnp.where(low, pltpu.roll(first, half, 1), second)
        after += jnp.where(lane == half, pltpu.roll(beyond, lanes - 8 * NC - c, 1), 0.0)
        out_ref[c, 0] = own + jnp.where(row > 0, pltpu.roll(after, 1, 0), 0.0)


def local(log_conf, brownian, relax_rate, kernel):
    comps, rows, ny, nz = log_conf.shape
    width_gx, width_gy = lax.axis_size("gx"), lax.axis_size("gy")
    planes = nz // 4
    assert comps == NC and rows == 4 and width_gy == 2 and width_gx % 2 == 0
    assert planes == width_gx * width_gy and ny == 256

    swap_first = [(i, i ^ 1) for i in range(width_gx)]
    swap_second = [(i, ((i + 1) ^ 1) - 1) for i in range(1, width_gx - 1)]
    cuts = [(0, ny // 2), (ny // 2, 7 * ny // 8), (7 * ny // 8, ny)]
    early = cuts[0][1]
    (first,) = pack(log_conf, early, False)
    second, cols = pack(log_conf, early, True)
    halos = [[lax.ppermute(first, "gx", swap_first), lax.ppermute(second, "gx", swap_second)]]
    cols = lax.ppermute(cols, "gy", [(0, 1), (1, 0)])
    begun, weights, pick, *sent = begin(log_conf, brownian, relax_rate, cols, kernel, cuts[1:])
    for first, second in zip(sent[0::2], sent[1::2]):
        halos.append([lax.ppermute(first, "gx", swap_first), lax.ppermute(second, "gx", swap_second)])

    part = None
    for (start, stop), pair in zip(cuts, halos):
        part = finish(start, stop, begun, pair, weights, pick, part)
    moved = lax.all_to_all(part.reshape(planes, 1, ROWS * ny // 2), ("gx", "gy"), 0, 0, tiled=True)
    return pl.pallas_call(
        gather_kernel,
        out_shape=jax.ShapeDtypeStruct((comps, 1, width_gx, ny // 2), jnp.float32),
        in_specs=[pl.BlockSpec(memory_space=pltpu.VMEM)],
        compiler_params=pltpu.CompilerParams(vmem_limit_bytes=4 * 2**20),
        name="gather",
    )(pltpu.with_memory_space_constraint(moved.reshape(planes * ROWS, ny // 2), pltpu.VMEM))


def solution(mesh):
    return jax.shard_map(
        local,
        mesh=mesh,
        in_specs=(
            P(None, ("grp", "gx"), "gy", None),
            P(None, ("grp", "gx"), "gy", None),
            P(("grp", "gx"), "gy", None),
            P(),
        ),
        out_specs=P(None, ("gx", "gy"), "grp", None),
        check_vma=False,
    )
```

```python
import functools

import jax
import jax.numpy as jnp
from jax import lax
from jax.experimental import pallas as pl
from jax.experimental.pallas import tpu as pltpu
from jax.sharding import PartitionSpec as P

STENCIL = 0.12 / 12.0
RELAX_STEP = 0.1
NOISE_AMP = 0.3
NC = 6
LANES = 128
ROWS = NC + 1
LEAD = 8
TAIL = 32


def band(size):
    row = lax.broadcasted_iota(jnp.int32, (size, size), 0)
    col = lax.broadcasted_iota(jnp.int32, (size, size), 1)
    gap = jnp.abs(row - col)
    value = jnp.where(gap == 0, -30.0, jnp.where(gap == 1, 16.0, jnp.where(gap == 2, -1.0, 0.0)))
    return value.astype(jnp.bfloat16)


def position():
    return lax.rem(lax.axis_index("gx"), 2), lax.axis_index("gy")


def pack_kernel(second, f_ref, *refs):
    odd, gy = position()
    comps, rows, ny, nz = f_ref.shape
    if second:
        out_ref, cols_ref, sems, edges, edge_sem = refs
    else:
        out_ref, sems = refs
    row = 2 * odd if second else 2 - 2 * odd
    copies = []
    copies.append(pltpu.make_async_copy(f_ref.at[:, pl.ds(row, 2), pl.ds(0, out_ref.shape[2])], out_ref, sems))
    if second:
        at = pl.multiple_of((1 - gy) * (ny - 16), 16)
        copies.append(pltpu.make_async_copy(f_ref.at[:, :, pl.ds(at, 16)], edges, edge_sem))
    for copy in copies:
        copy.start()
    for copy in copies:
        copy.wait()
    if second:
        for c in range(comps):
            for x in range(rows):
                values = edges[c, x].astype(jnp.float32)
                cols_ref[c, x] = jnp.where(gy == 0, values[14:16], values[0:2])


def pack(log_conf, stop, second):
    comps, rows, ny, nz = log_conf.shape
    shapes = [jax.ShapeDtypeStruct((comps, 2, stop, nz), log_conf.dtype)]
    scratch = [pltpu.SemaphoreType.DMA]
    if second:
        shapes.append(jax.ShapeDtypeStruct((comps, rows, 2, nz), jnp.float32))
        scratch += [pltpu.VMEM((comps, rows, 16, nz), log_conf.dtype), pltpu.SemaphoreType.DMA]
    return pl.pallas_call(
        functools.partial(pack_kernel, second),
        in_specs=[pl.BlockSpec(memory_space=pltpu.HBM)],
        out_specs=[pl.BlockSpec(memory_space=pltpu.VMEM)] * len(shapes),
        out_shape=shapes,
        scratch_shapes=scratch,
        compiler_params=pltpu.CompilerParams(vmem_limit_bytes=4 * 2**20),
        name="pack",
    )(pltpu.with_memory_space_constraint(log_conf, pltpu.HBM))


def begin_kernel(
    cuts, f_ref, b_ref, r_ref, cols_ref, k_ref, out_ref, w_ref, pick_ref, *refs
):
    rows, ny = f_ref.shape[1], f_ref.shape[2]
    odd, gy = position()
    ty_ref, tz_ref = refs[-2:]
    step = 64

    @pl.when(pl.program_id(0) == 0)
    def _():
        nz = f_ref.shape[3]
        ty_ref[...] = band(ny)
        tz_ref[...] = band(nz)
        planes = pick_ref.shape[0]
        z = lax.broadcasted_iota(jnp.int32, (planes, nz), 1)
        k = lax.broadcasted_iota(jnp.int32, (planes, nz), 0)
        for piece, chosen in enumerate((lax.shift_right_logical(z + 2, 2) == k, z == 4 * k + 2)):
            value = jnp.where(chosen, 1.0, 0.0).astype(jnp.bfloat16)
            pick_ref[:, piece * nz : (piece + 1) * nz] = value
            pick_ref[:, (piece + 2) * nz : (piece + 3) * nz] = value
        tap = (lax.broadcasted_iota(jnp.int32, (NC, nz), 1) + 2) & 3
        for a in range(5):
            for b in range(5):
                taps = k_ref[a, b]
                near = jnp.broadcast_to(taps[:, 0:1], (NC, nz))
                for e in range(1, 4):
                    near = jnp.where(tap == e, taps[:, e : e + 1], near)
                w_ref[a, b, 0] = near
                w_ref[a, b, 1] = jnp.broadcast_to(taps[:, 4:5], (NC, nz))

    for (start, stop), first_ref, second_ref in zip(cuts, refs[0:-2:2], refs[1:-2:2]):
        first_ref[0] = f_ref[0, pl.ds(2 - 2 * odd, 2), start:stop]
        second_ref[0] = f_ref[0, pl.ds(2 * odd, 2), start:stop]
    for x in range(rows):
        plane = f_ref[0, x]
        for y in range(0, ny, step):
            ys = pl.ds(y, step)
            part = f_ref[0, x, ys]
            lap = jnp.dot(ty_ref[ys], plane, preferred_element_type=jnp.float32)
            lap += jnp.dot(part, tz_ref[...], preferred_element_type=jnp.float32)
            own = part.astype(jnp.float32)
            lap -= 30.0 * own
            for other in range(rows):
                if abs(other - x) == 1:
                    lap += 16.0 * f_ref[0, other, ys].astype(jnp.float32)
                elif abs(other - x) == 2:
                    lap -= f_ref[0, other, ys].astype(jnp.float32)
            rate = r_ref[x, ys].astype(jnp.float32)
            noise = b_ref[0, x, ys].astype(jnp.float32)
            out_ref[0, x, ys] = own - RELAX_STEP * rate * own + NOISE_AMP * noise + STENCIL * lap
        near_row = lax.broadcasted_iota(jnp.int32, (8, 1), 0)
        first = cols_ref[0, x, 0:1]
        second = cols_ref[0, x, 1:2]

        @pl.when(gy == 1)
        def _():
            extra = jnp.where(near_row == 0, 16.0 * second - first, jnp.where(near_row == 1, -second, 0.0))
            out_ref[0, x, 0:8] += STENCIL * extra

        @pl.when(gy == 0)
        def _():
            extra = jnp.where(near_row == 7, 16.0 * first - second, jnp.where(near_row == 6, -first, 0.0))
            out_ref[0, x, ny - 8 : ny] += STENCIL * extra


def begin(log_conf, brownian, relax_rate, cols, kernel, cuts):
    comps, rows, ny, nz = log_conf.shape
    whole = lambda *shape: pl.BlockSpec(shape, lambda c: (0,) * len(shape))
    block = pl.BlockSpec((1, rows, ny, nz), lambda c: (c, 0, 0, 0))
    heights = [stop - start for start, stop in cuts for _ in range(2)]
    return pl.pallas_call(
        functools.partial(begin_kernel, cuts),
        grid=(comps,),
        in_specs=[
            block,
            block,
            whole(rows, ny, nz),
            pl.BlockSpec((1, rows, 2, nz), lambda c: (c, 0, 0, 0)),
            whole(5, 5, comps, 5),
        ],
        out_specs=[block, whole(5, 5, 2, comps, nz), whole(nz // 4, 4 * nz)]
        + [pl.BlockSpec((1, 2, height, nz), lambda c: (c, 0, 0, 0)) for height in heights],
        out_shape=[
            jax.ShapeDtypeStruct((comps, rows, ny, nz), jnp.float32),
            jax.ShapeDtypeStruct((5, 5, 2, comps, nz), jnp.float32),
            jax.ShapeDtypeStruct((nz // 4, 4 * nz), jnp.bfloat16),
        ]
        + [jax.ShapeDtypeStruct((comps, 2, height, nz), log_conf.dtype) for height in heights],
        scratch_shapes=[pltpu.VMEM((ny, ny), jnp.bfloat16), pltpu.VMEM((nz, nz), jnp.bfloat16)],
        compiler_params=pltpu.CompilerParams(vmem_limit_bytes=16 * 2**20),
        cost_estimate=pl.CostEstimate(
            flops=30 * comps * rows * ny * nz, bytes_accessed=10 * comps * rows * ny * nz, transcendentals=0
        ),
        name="begin",
    )(*(pltpu.with_memory_space_constraint(x, pltpu.HBM) for x in (log_conf, brownian, relax_rate)), cols, jnp.transpose(kernel, (1, 2, 0, 3)))


def finish_kernel(start, stop, has_base, u_ref, a_ref, b_ref, w_ref, pick_ref, *refs):
    if has_base:
        base_ref, out_ref, stress, sums = refs
    else:
        out_ref, stress, sums = refs
    rows, ny, nz = u_ref.shape[1:]
    width, nj = stop - start, ny // 4
    own_j, planes, pieces = width // 4, out_ref.shape[0] // ROWS, nz // LANES
    first_ref, second_ref = (b_ref, a_ref) if start > 3 * u_ref.shape[2] // 4 else (a_ref, b_ref)
    odd, _ = position()
    compact = len(sums.shape) == 2
    if compact:
        for t in range(2):
            sums[t * nj + 8 * NC : (t + 1) * nj] = jnp.zeros((nj - 8 * NC, 2 * nz), jnp.float32)
    for c in range(NC):
        for r in range(rows):
            for piece in range(pieces):
                stress[c, r, piece, 0:LEAD] = jnp.zeros((LEAD, LANES), jnp.float32)
                if not compact:
                    stress[c, r, piece, LEAD + width :] = jnp.zeros((TAIL, LANES), jnp.float32)

    for side, halo_ref in enumerate((first_ref, second_ref)):
        upper = (odd == side).astype(jnp.int32)
        near, far = 1 - upper, upper
        edge, inner = 3 * upper, 1 + upper

        def chunk(step, carry, halo_ref=halo_ref, near=near, far=far, edge=edge, inner=inner):
            y = pl.multiple_of(step * 16, 16)
            ys, us = pl.ds(y, 16), pl.ds(start + y, 16)
            updated = ([], [])
            for c in range(NC):
                close = halo_ref[c, near, ys].astype(jnp.float32)
                distant = halo_ref[c, far, ys].astype(jnp.float32)
                updated[0].append(u_ref[c, inner, us] - STENCIL * close)
                updated[1].append(u_ref[c, edge, us] + (16.0 * STENCIL) * close - STENCIL * distant)
            for row, (xx, xy, xz, yy, yz, zz) in zip((inner, edge), updated):
                xy2, xz2, yz2 = xy * xy, xz * xz, yz * yz
                values = (
                    xx + 0.5 * (xx * xx + xy2 + xz2),
                    xy + 0.5 * (xy * (xx + yy) + xz * yz),
                    xz + 0.5 * (xz * (xx + zz) + xy * yz),
                    yy + 0.5 * (xy2 + yy * yy + yz2),
                    yz + 0.5 * (yz * (yy + zz) + xy * xz),
                    zz + 0.5 * (xz2 + yz2 + zz * zz),
                )
                for c in range(NC):
                    for piece in range(pieces):
                        lanes = slice(piece * LANES, (piece + 1) * LANES)
                        stress[c, row, piece, pl.ds(y + LEAD, 16)] = values[c][:, lanes]
            return carry

        lax.fori_loop(0, width // 16, chunk, 0)

    taps = {0: ((0, 2), (1, 3), (2, 4)), 1: ((2, 0), (3, 1))}
    for c in range(NC):
        for t in range(2):
            weight = {}
            for row, a in taps[t]:
                for b in range(5):
                    for k in range(2):
                        weight[row, b, k] = w_ref[a, b, k, c : c + 1]
            for jb in range(own_j // 8 + 1):
                total = [None, None]
                for b in range(5 if jb < own_j // 8 else 2):
                    at = pl.ds(LEAD + 32 * jb + b - 2, 8, stride=4)
                    for row, _ in taps[t]:
                        value = jnp.concatenate([stress[c, row, piece, at] for piece in range(pieces)], axis=1)
                        for k in range(2):
                            term = value * weight[row, b, k]
                            total[k] = term if total[k] is None else total[k] + term
                for k in range(2):
                    lanes = slice(k * nz, (k + 1) * nz)
                    if not compact:
                        sums[c, t, 8 * jb : 8 * jb + 8, lanes] = total[k]
                    elif jb == 0:
                        sums[t * nj + 8 * c : t * nj + 8 * c + 8, lanes] = total[k]
                    else:
                        at = t * nj + 8 * NC + c
                        sums[at : at + 1, lanes] = total[k][0:1]

    def reduced(values):
        high = values.astype(jnp.bfloat16)
        low = (values - high.astype(jnp.float32)).astype(jnp.bfloat16)
        both = jnp.concatenate([high, low], axis=1)
        return lax.dot_general(
            pick_ref[...], both, (((1,), (1,)), ((), ())), preferred_element_type=jnp.float32
        )

    def put(place, value):
        at = pl.ds(place, planes, stride=ROWS)
        if has_base:
            value = value + base_ref[at, :]
        out_ref[at, :] = value

    if compact:
        lane = lax.broadcasted_iota(jnp.int32, (planes, 2 * nj), 1)
        spread = reduced(sums[...])
        for c in range(NC):
            moved = pltpu.roll(spread, nj - 8 - 8 * c, 1)
            put(c, jnp.where((lane & (nj - 1)) >= nj - 8, moved, 0.0))
        out_ref[pl.ds(NC, planes, stride=ROWS), :] = spread
        return

    first_j = start // 4
    held = min(own_j + 8, nj - first_j)
    for c in range(NC):
        parts = []
        for t in range(2):
            if first_j:
                parts.append(jnp.zeros((first_j, 2 * nz), jnp.float32))
            parts.append(sums[c, t, 0:held])
            if first_j + held < nj:
                parts.append(jnp.zeros((nj - first_j - held, 2 * nz), jnp.float32))
        put(c, reduced(jnp.concatenate(parts, axis=0)))
    out_ref[pl.ds(NC, planes, stride=ROWS), :] = jnp.zeros((planes, 2 * nj), jnp.float32)


def finish(start, stop, begun, halos, weights, pick, base):
    comps, rows, ny, nz = begun.shape
    planes, nj = nz // 4, ny // 4
    places = (2 * nj, 2 * nz) if stop == ny else (comps, 2, (stop - start) // 4 + 8, 2 * nz)
    operands = [begun, *(halos[::-1] if start > 3 * begun.shape[2] // 4 else halos), weights, pick] + ([] if base is None else [base])
    operands = [pltpu.with_memory_space_constraint(x, pltpu.VMEM) for x in operands]
    return pl.pallas_call(
        functools.partial(finish_kernel, start, stop, base is not None),
        in_specs=[pl.BlockSpec(memory_space=pltpu.VMEM)] * len(operands),
        out_specs=pl.BlockSpec(memory_space=pltpu.VMEM),
        out_shape=jax.ShapeDtypeStruct((planes * ROWS, 2 * nj), jnp.float32),
        scratch_shapes=[
            pltpu.VMEM((comps, rows, nz // LANES, LEAD + stop - start + TAIL, LANES), jnp.float32),
            pltpu.VMEM(places, jnp.float32),
        ],
        compiler_params=pltpu.CompilerParams(vmem_limit_bytes=16 * 2**20),
        cost_estimate=pl.CostEstimate(
            flops=80 * comps * (stop - start) * nz, bytes_accessed=32 * comps * (stop - start) * nz, transcendentals=0
        ),
        name="finish",
    )(*operands)


def gather_kernel(in_ref, out_ref):
    count, lanes = out_ref.shape[2], out_ref.shape[3]
    half = lanes // 2
    lane = lax.broadcasted_iota(jnp.int32, (count, lanes), 1)
    row = lax.broadcasted_iota(jnp.int32, (count, lanes), 0)
    low = lane < half
    beyond = in_ref[pl.ds(NC, count, stride=2 * ROWS), :]
    for c in range(NC):
        first = in_ref[pl.ds(c, count, stride=2 * ROWS), :]
        second = in_ref[pl.ds(ROWS + c, count, stride=2 * ROWS), :]
        own = jnp.where(low, first, pltpu.roll(second, half, 1))
        own += jnp.where(lane == half, pltpu.roll(beyond, half - 8 * NC - c, 1), 0.0)
        after = jnp.where(low, pltpu.roll(first, half, 1), second)
        after += jnp.where(lane == half, pltpu.roll(beyond, lanes - 8 * NC - c, 1), 0.0)
        out_ref[c, 0] = own + jnp.where(row > 0, pltpu.roll(after, 1, 0), 0.0)


def local(log_conf, brownian, relax_rate, kernel):
    comps, rows, ny, nz = log_conf.shape
    width_gx, width_gy = lax.axis_size("gx"), lax.axis_size("gy")
    planes = nz // 4
    assert comps == NC and rows == 4 and width_gy == 2 and width_gx % 2 == 0
    assert planes == width_gx * width_gy and ny == 256

    swap_first = [(i, i ^ 1) for i in range(width_gx)]
    swap_second = [(i, ((i + 1) ^ 1) - 1) for i in range(1, width_gx - 1)]
    cuts = [(0, 5 * ny // 8), (5 * ny // 8, 7 * ny // 8), (7 * ny // 8, ny)]
    early = cuts[0][1]
    (first,) = pack(log_conf, early, False)
    second, cols = pack(log_conf, early, True)
    halos = [[lax.ppermute(first, "gx", swap_first), lax.ppermute(second, "gx", swap_second)]]
    cols = lax.ppermute(cols, "gy", [(0, 1), (1, 0)])
    begun, weights, pick, *sent = begin(log_conf, brownian, relax_rate, cols, kernel, cuts[1:])
    for first, second in zip(sent[0::2], sent[1::2]):
        halos.append([lax.ppermute(first, "gx", swap_first), lax.ppermute(second, "gx", swap_second)])

    part = None
    for (start, stop), pair in zip(cuts, halos):
        part = finish(start, stop, begun, pair, weights, pick, part)
    moved = lax.all_to_all(part.reshape(planes, 1, ROWS * ny // 2), ("gx", "gy"), 0, 0, tiled=True)
    return pl.pallas_call(
        gather_kernel,
        out_shape=jax.ShapeDtypeStruct((comps, 1, width_gx, ny // 2), jnp.float32),
        in_specs=[pl.BlockSpec(memory_space=pltpu.VMEM)],
        compiler_params=pltpu.CompilerParams(vmem_limit_bytes=4 * 2**20),
        name="gather",
    )(pltpu.with_memory_space_constraint(moved.reshape(planes * ROWS, ny // 2), pltpu.VMEM))


def solution(mesh):
    return jax.shard_map(
        local,
        mesh=mesh,
        in_specs=(
            P(None, ("grp", "gx"), "gy", None),
            P(None, ("grp", "gx"), "gy", None),
            P(("grp", "gx"), "gy", None),
            P(),
        ),
        out_specs=P(None, ("gx", "gy"), "grp", None),
        check_vma=False,
    )
```

```python
import functools

import jax
import jax.numpy as jnp
from jax import lax
from jax.experimental import pallas as pl
from jax.experimental.pallas import tpu as pltpu
from jax.sharding import PartitionSpec as P

STENCIL = 0.12 / 12.0
RELAX_STEP = 0.1
NOISE_AMP = 0.3
NC = 6
LANES = 128
ROWS = NC + 1
LEAD = 8
TAIL = 32


def band(size):
    row = lax.broadcasted_iota(jnp.int32, (size, size), 0)
    col = lax.broadcasted_iota(jnp.int32, (size, size), 1)
    gap = jnp.abs(row - col)
    value = jnp.where(gap == 0, -30.0, jnp.where(gap == 1, 16.0, jnp.where(gap == 2, -1.0, 0.0)))
    return value.astype(jnp.bfloat16)


def position():
    return lax.rem(lax.axis_index("gx"), 2), lax.axis_index("gy")


def pack_kernel(second, f_ref, *refs):
    odd, gy = position()
    comps, rows, ny, nz = f_ref.shape
    if second:
        out_ref, cols_ref, sems, edges, edge_sem = refs
    else:
        out_ref, sems = refs
    row = 2 * odd if second else 2 - 2 * odd
    copies = []
    copies.append(pltpu.make_async_copy(f_ref.at[:, pl.ds(row, 2), pl.ds(0, out_ref.shape[2])], out_ref, sems))
    if second:
        at = pl.multiple_of((1 - gy) * (ny - 16), 16)
        copies.append(pltpu.make_async_copy(f_ref.at[:, :, pl.ds(at, 16)], edges, edge_sem))
    for copy in copies:
        copy.start()
    for copy in copies:
        copy.wait()
    if second:
        for c in range(comps):
            for x in range(rows):
                values = edges[c, x].astype(jnp.float32)
                cols_ref[c, x] = jnp.where(gy == 0, values[14:16], values[0:2])


def pack(log_conf, stop, second):
    comps, rows, ny, nz = log_conf.shape
    shapes = [jax.ShapeDtypeStruct((comps, 2, stop, nz), log_conf.dtype)]
    scratch = [pltpu.SemaphoreType.DMA]
    if second:
        shapes.append(jax.ShapeDtypeStruct((comps, rows, 2, nz), jnp.float32))
        scratch += [pltpu.VMEM((comps, rows, 16, nz), log_conf.dtype), pltpu.SemaphoreType.DMA]
    return pl.pallas_call(
        functools.partial(pack_kernel, second),
        in_specs=[pl.BlockSpec(memory_space=pltpu.HBM)],
        out_specs=[pl.BlockSpec(memory_space=pltpu.VMEM)] * len(shapes),
        out_shape=shapes,
        scratch_shapes=scratch,
        compiler_params=pltpu.CompilerParams(vmem_limit_bytes=4 * 2**20),
        name="pack",
    )(pltpu.with_memory_space_constraint(log_conf, pltpu.HBM))


def begin_kernel(
    cuts, f_ref, b_ref, r_ref, cols_ref, k_ref, out_ref, w_ref, pick_ref, *refs
):
    rows, ny = f_ref.shape[1], f_ref.shape[2]
    odd, gy = position()
    ty_ref, tz_ref = refs[-2:]
    step = 64

    @pl.when(pl.program_id(0) == 0)
    def _():
        nz = f_ref.shape[3]
        ty_ref[...] = band(ny)
        tz_ref[...] = band(nz)
        planes = pick_ref.shape[0]
        z = lax.broadcasted_iota(jnp.int32, (planes, nz), 1)
        k = lax.broadcasted_iota(jnp.int32, (planes, nz), 0)
        for piece, chosen in enumerate((lax.shift_right_logical(z + 2, 2) == k, z == 4 * k + 2)):
            value = jnp.where(chosen, 1.0, 0.0).astype(jnp.bfloat16)
            pick_ref[:, piece * nz : (piece + 1) * nz] = value
            pick_ref[:, (piece + 2) * nz : (piece + 3) * nz] = value
        tap = (lax.broadcasted_iota(jnp.int32, (NC, nz), 1) + 2) & 3
        for a in range(5):
            for b in range(5):
                taps = k_ref[a, b]
                near = jnp.broadcast_to(taps[:, 0:1], (NC, nz))
                for e in range(1, 4):
                    near = jnp.where(tap == e, taps[:, e : e + 1], near)
                w_ref[a, b, 0] = near
                w_ref[a, b, 1] = jnp.broadcast_to(taps[:, 4:5], (NC, nz))

    for (start, stop), first_ref, second_ref in zip(cuts, refs[0:-2:2], refs[1:-2:2]):
        first_ref[0] = f_ref[0, pl.ds(2 - 2 * odd, 2), start:stop]
        second_ref[0] = f_ref[0, pl.ds(2 * odd, 2), start:stop]
    for x in range(rows):
        plane = f_ref[0, x]
        for y in range(0, ny, step):
            ys = pl.ds(y, step)
            part = f_ref[0, x, ys]
            lap = jnp.dot(ty_ref[ys], plane, preferred_element_type=jnp.float32)
            lap += jnp.dot(part, tz_ref[...], preferred_element_type=jnp.float32)
            own = part.astype(jnp.float32)
            lap -= 30.0 * own
            for other in range(rows):
                if abs(other - x) == 1:
                    lap += 16.0 * f_ref[0, other, ys].astype(jnp.float32)
                elif abs(other - x) == 2:
                    lap -= f_ref[0, other, ys].astype(jnp.float32)
            rate = r_ref[x, ys].astype(jnp.float32)
            noise = b_ref[0, x, ys].astype(jnp.float32)
            out_ref[0, x, ys] = own - RELAX_STEP * rate * own + NOISE_AMP * noise + STENCIL * lap
        near_row = lax.broadcasted_iota(jnp.int32, (8, 1), 0)
        first = cols_ref[0, x, 0:1]
        second = cols_ref[0, x, 1:2]

        @pl.when(gy == 1)
        def _():
            extra = jnp.where(near_row == 0, 16.0 * second - first, jnp.where(near_row == 1, -second, 0.0))
            out_ref[0, x, 0:8] += STENCIL * extra

        @pl.when(gy == 0)
        def _():
            extra = jnp.where(near_row == 7, 16.0 * first - second, jnp.where(near_row == 6, -first, 0.0))
            out_ref[0, x, ny - 8 : ny] += STENCIL * extra


def begin(log_conf, brownian, relax_rate, cols, kernel, cuts):
    comps, rows, ny, nz = log_conf.shape
    whole = lambda *shape: pl.BlockSpec(shape, lambda c: (0,) * len(shape))
    block = pl.BlockSpec((1, rows, ny, nz), lambda c: (c, 0, 0, 0))
    heights = [stop - start for start, stop in cuts for _ in range(2)]
    return pl.pallas_call(
        functools.partial(begin_kernel, cuts),
        grid=(comps,),
        in_specs=[
            block,
            block,
            whole(rows, ny, nz),
            pl.BlockSpec((1, rows, 2, nz), lambda c: (c, 0, 0, 0)),
            whole(5, 5, comps, 5),
        ],
        out_specs=[block, whole(5, 5, 2, comps, nz), whole(nz // 4, 4 * nz)]
        + [pl.BlockSpec((1, 2, height, nz), lambda c: (c, 0, 0, 0)) for height in heights],
        out_shape=[
            jax.ShapeDtypeStruct((comps, rows, ny, nz), jnp.float32),
            jax.ShapeDtypeStruct((5, 5, 2, comps, nz), jnp.float32),
            jax.ShapeDtypeStruct((nz // 4, 4 * nz), jnp.bfloat16),
        ]
        + [jax.ShapeDtypeStruct((comps, 2, height, nz), log_conf.dtype) for height in heights],
        scratch_shapes=[pltpu.VMEM((ny, ny), jnp.bfloat16), pltpu.VMEM((nz, nz), jnp.bfloat16)],
        compiler_params=pltpu.CompilerParams(vmem_limit_bytes=16 * 2**20),
        cost_estimate=pl.CostEstimate(
            flops=30 * comps * rows * ny * nz, bytes_accessed=10 * comps * rows * ny * nz, transcendentals=0
        ),
        name="begin",
    )(*(pltpu.with_memory_space_constraint(x, pltpu.HBM) for x in (log_conf, brownian, relax_rate)), cols, jnp.transpose(kernel, (1, 2, 0, 3)))


def finish_kernel(start, stop, has_base, u_ref, a_ref, b_ref, w_ref, pick_ref, *refs):
    if has_base:
        base_ref, out_ref, stress, sums = refs
    else:
        out_ref, stress, sums = refs
    rows, ny, nz = u_ref.shape[1:]
    width, nj = stop - start, ny // 4
    own_j, planes, pieces = width // 4, out_ref.shape[0] // ROWS, nz // LANES
    first_ref, second_ref = (b_ref, a_ref) if start > 3 * u_ref.shape[2] // 4 else (a_ref, b_ref)
    odd, _ = position()
    compact = len(sums.shape) == 2
    if compact:
        for t in range(2):
            sums[t * nj + 8 * NC : (t + 1) * nj] = jnp.zeros((nj - 8 * NC, 2 * nz), jnp.float32)
    for c in range(NC):
        for r in range(rows):
            for piece in range(pieces):
                stress[c, r, piece, 0:LEAD] = jnp.zeros((LEAD, LANES), jnp.float32)
                if not compact:
                    stress[c, r, piece, LEAD + width :] = jnp.zeros((TAIL, LANES), jnp.float32)

    for side, halo_ref in enumerate((first_ref, second_ref)):
        upper = (odd == side).astype(jnp.int32)
        near, far = 1 - upper, upper
        edge, inner = 3 * upper, 1 + upper

        def chunk(step, carry, halo_ref=halo_ref, near=near, far=far, edge=edge, inner=inner):
            y = pl.multiple_of(step * 16, 16)
            ys, us = pl.ds(y, 16), pl.ds(start + y, 16)
            updated = ([], [])
            for c in range(NC):
                close = halo_ref[c, near, ys].astype(jnp.float32)
                distant = halo_ref[c, far, ys].astype(jnp.float32)
                updated[0].append(u_ref[c, inner, us] - STENCIL * close)
                updated[1].append(u_ref[c, edge, us] + (16.0 * STENCIL) * close - STENCIL * distant)
            for row, (xx, xy, xz, yy, yz, zz) in zip((inner, edge), updated):
                xy2, xz2, yz2 = xy * xy, xz * xz, yz * yz
                values = (
                    xx + 0.5 * (xx * xx + xy2 + xz2),
                    xy + 0.5 * (xy * (xx + yy) + xz * yz),
                    xz + 0.5 * (xz * (xx + zz) + xy * yz),
                    yy + 0.5 * (xy2 + yy * yy + yz2),
                    yz + 0.5 * (yz * (yy + zz) + xy * xz),
                    zz + 0.5 * (xz2 + yz2 + zz * zz),
                )
                for c in range(NC):
                    for piece in range(pieces):
                        lanes = slice(piece * LANES, (piece + 1) * LANES)
                        stress[c, row, piece, pl.ds(y + LEAD, 16)] = values[c][:, lanes]
            return carry

        lax.fori_loop(0, width // 16, chunk, 0)

    taps = {0: ((0, 2), (1, 3), (2, 4)), 1: ((2, 0), (3, 1))}
    for c in range(NC):
        weight = {}
        for t in range(2):
            for row, a in taps[t]:
                for b in range(5):
                    for k in range(2):
                        weight[t, row, b, k] = w_ref[a, b, k, c : c + 1]
        for jb in range(own_j // 8 + 1):
            total = {}
            for b in range(5 if jb < own_j // 8 else 2):
                at = pl.ds(LEAD + 32 * jb + b - 2, 8, stride=4)
                for row in range(rows):
                    value = jnp.concatenate([stress[c, row, piece, at] for piece in range(pieces)], axis=1)
                    for t in range(2):
                        for k in range(2):
                            if (t, row, b, k) in weight:
                                term = value * weight[t, row, b, k]
                                total[t, k] = total[t, k] + term if (t, k) in total else term
            for t in range(2):
                for k in range(2):
                    lanes = slice(k * nz, (k + 1) * nz)
                    if not compact:
                        sums[c, t, 8 * jb : 8 * jb + 8, lanes] = total[t, k]
                    elif jb == 0:
                        sums[t * nj + 8 * c : t * nj + 8 * c + 8, lanes] = total[t, k]
                    else:
                        at = t * nj + 8 * NC + c
                        sums[at : at + 1, lanes] = total[t, k][0:1]

    def reduced(values):
        high = values.astype(jnp.bfloat16)
        low = (values - high.astype(jnp.float32)).astype(jnp.bfloat16)
        both = jnp.concatenate([high, low], axis=1)
        return lax.dot_general(
            pick_ref[...], both, (((1,), (1,)), ((), ())), preferred_element_type=jnp.float32
        )

    def put(place, value):
        at = pl.ds(place, planes, stride=ROWS)
        if has_base:
            value = value + base_ref[at, :]
        out_ref[at, :] = value

    if compact:
        lane = lax.broadcasted_iota(jnp.int32, (planes, 2 * nj), 1)
        spread = reduced(sums[...])
        for c in range(NC):
            moved = pltpu.roll(spread, nj - 8 - 8 * c, 1)
            put(c, jnp.where((lane & (nj - 1)) >= nj - 8, moved, 0.0))
        out_ref[pl.ds(NC, planes, stride=ROWS), :] = spread
        return

    first_j = start // 4
    held = min(own_j + 8, nj - first_j)
    for c in range(NC):
        parts = []
        for t in range(2):
            if first_j:
                parts.append(jnp.zeros((first_j, 2 * nz), jnp.float32))
            parts.append(sums[c, t, 0:held])
            if first_j + held < nj:
                parts.append(jnp.zeros((nj - first_j - held, 2 * nz), jnp.float32))
        put(c, reduced(jnp.concatenate(parts, axis=0)))
    out_ref[pl.ds(NC, planes, stride=ROWS), :] = jnp.zeros((planes, 2 * nj), jnp.float32)


def finish(start, stop, begun, halos, weights, pick, base):
    comps, rows, ny, nz = begun.shape
    planes, nj = nz // 4, ny // 4
    places = (2 * nj, 2 * nz) if stop == ny else (comps, 2, (stop - start) // 4 + 8, 2 * nz)
    operands = [begun, *(halos[::-1] if start > 3 * begun.shape[2] // 4 else halos), weights, pick] + ([] if base is None else [base])
    operands = [pltpu.with_memory_space_constraint(x, pltpu.VMEM) for x in operands]
    return pl.pallas_call(
        functools.partial(finish_kernel, start, stop, base is not None),
        in_specs=[pl.BlockSpec(memory_space=pltpu.VMEM)] * len(operands),
        out_specs=pl.BlockSpec(memory_space=pltpu.VMEM),
        out_shape=jax.ShapeDtypeStruct((planes * ROWS, 2 * nj), jnp.float32),
        scratch_shapes=[
            pltpu.VMEM((comps, rows, nz // LANES, LEAD + stop - start + TAIL, LANES), jnp.float32),
            pltpu.VMEM(places, jnp.float32),
        ],
        compiler_params=pltpu.CompilerParams(vmem_limit_bytes=16 * 2**20),
        cost_estimate=pl.CostEstimate(
            flops=80 * comps * (stop - start) * nz, bytes_accessed=32 * comps * (stop - start) * nz, transcendentals=0
        ),
        name="finish",
    )(*operands)


def gather_kernel(in_ref, out_ref):
    count, lanes = out_ref.shape[2], out_ref.shape[3]
    half = lanes // 2
    lane = lax.broadcasted_iota(jnp.int32, (count, lanes), 1)
    row = lax.broadcasted_iota(jnp.int32, (count, lanes), 0)
    low = lane < half
    beyond = in_ref[pl.ds(NC, count, stride=2 * ROWS), :]
    for c in range(NC):
        first = in_ref[pl.ds(c, count, stride=2 * ROWS), :]
        second = in_ref[pl.ds(ROWS + c, count, stride=2 * ROWS), :]
        own = jnp.where(low, first, pltpu.roll(second, half, 1))
        own += jnp.where(lane == half, pltpu.roll(beyond, half - 8 * NC - c, 1), 0.0)
        after = jnp.where(low, pltpu.roll(first, half, 1), second)
        after += jnp.where(lane == half, pltpu.roll(beyond, lanes - 8 * NC - c, 1), 0.0)
        out_ref[c, 0] = own + jnp.where(row > 0, pltpu.roll(after, 1, 0), 0.0)


def local(log_conf, brownian, relax_rate, kernel):
    comps, rows, ny, nz = log_conf.shape
    width_gx, width_gy = lax.axis_size("gx"), lax.axis_size("gy")
    planes = nz // 4
    assert comps == NC and rows == 4 and width_gy == 2 and width_gx % 2 == 0
    assert planes == width_gx * width_gy and ny == 256

    swap_first = [(i, i ^ 1) for i in range(width_gx)]
    swap_second = [(i, ((i + 1) ^ 1) - 1) for i in range(1, width_gx - 1)]
    cuts = [(0, 5 * ny // 8), (5 * ny // 8, 7 * ny // 8), (7 * ny // 8, ny)]
    early = cuts[0][1]
    (first,) = pack(log_conf, early, False)
    second, cols = pack(log_conf, early, True)
    halos = [[lax.ppermute(first, "gx", swap_first), lax.ppermute(second, "gx", swap_second)]]
    cols = lax.ppermute(cols, "gy", [(0, 1), (1, 0)])
    begun, weights, pick, *sent = begin(log_conf, brownian, relax_rate, cols, kernel, cuts[1:])
    for first, second in zip(sent[0::2], sent[1::2]):
        halos.append([lax.ppermute(first, "gx", swap_first), lax.ppermute(second, "gx", swap_second)])

    part = None
    for (start, stop), pair in zip(cuts, halos):
        part = finish(start, stop, begun, pair, weights, pick, part)
    moved = lax.all_to_all(part.reshape(planes, 1, ROWS * ny // 2), ("gx", "gy"), 0, 0, tiled=True)
    return pl.pallas_call(
        gather_kernel,
        out_shape=jax.ShapeDtypeStruct((comps, 1, width_gx, ny // 2), jnp.float32),
        in_specs=[pl.BlockSpec(memory_space=pltpu.VMEM)],
        compiler_params=pltpu.CompilerParams(vmem_limit_bytes=4 * 2**20),
        name="gather",
    )(pltpu.with_memory_space_constraint(moved.reshape(planes * ROWS, ny // 2), pltpu.VMEM))


def solution(mesh):
    return jax.shard_map(
        local,
        mesh=mesh,
        in_specs=(
            P(None, ("grp", "gx"), "gy", None),
            P(None, ("grp", "gx"), "gy", None),
            P(("grp", "gx"), "gy", None),
            P(),
        ),
        out_specs=P(None, ("gx", "gy"), "grp", None),
        check_vma=False,
    )
```

```python
import functools

import jax
import jax.numpy as jnp
from jax import lax
from jax.experimental import pallas as pl
from jax.experimental.pallas import tpu as pltpu
from jax.sharding import PartitionSpec as P

STENCIL = 0.12 / 12.0
RELAX_STEP = 0.1
NOISE_AMP = 0.3
NC = 6
LANES = 128
ROWS = NC + 1
LEAD = 8
TAIL = 32


def band(size):
    row = lax.broadcasted_iota(jnp.int32, (size, size), 0)
    col = lax.broadcasted_iota(jnp.int32, (size, size), 1)
    gap = jnp.abs(row - col)
    value = jnp.where(gap == 0, -30.0, jnp.where(gap == 1, 16.0, jnp.where(gap == 2, -1.0, 0.0)))
    return value.astype(jnp.bfloat16)


def position():
    return lax.rem(lax.axis_index("gx"), 2), lax.axis_index("gy")


def pack_kernel(second, f_ref, *refs):
    odd, gy = position()
    comps, rows, ny, nz = f_ref.shape
    if second:
        out_ref, cols_ref, sems, edges, edge_sem = refs
    else:
        out_ref, sems = refs
    row = 2 * odd if second else 2 - 2 * odd
    copies = []
    copies.append(pltpu.make_async_copy(f_ref.at[:, pl.ds(row, 2), pl.ds(0, out_ref.shape[2])], out_ref, sems))
    if second:
        at = pl.multiple_of((1 - gy) * (ny - 16), 16)
        copies.append(pltpu.make_async_copy(f_ref.at[:, :, pl.ds(at, 16)], edges, edge_sem))
    for copy in copies:
        copy.start()
    for copy in copies:
        copy.wait()
    if second:
        for c in range(comps):
            for x in range(rows):
                values = edges[c, x].astype(jnp.float32)
                cols_ref[c, x] = jnp.where(gy == 0, values[14:16], values[0:2])


def pack(log_conf, stop, second):
    comps, rows, ny, nz = log_conf.shape
    shapes = [jax.ShapeDtypeStruct((comps, 2, stop, nz), log_conf.dtype)]
    scratch = [pltpu.SemaphoreType.DMA]
    if second:
        shapes.append(jax.ShapeDtypeStruct((comps, rows, 2, nz), jnp.float32))
        scratch += [pltpu.VMEM((comps, rows, 16, nz), log_conf.dtype), pltpu.SemaphoreType.DMA]
    return pl.pallas_call(
        functools.partial(pack_kernel, second),
        in_specs=[pl.BlockSpec(memory_space=pltpu.HBM)],
        out_specs=[pl.BlockSpec(memory_space=pltpu.VMEM)] * len(shapes),
        out_shape=shapes,
        scratch_shapes=scratch,
        compiler_params=pltpu.CompilerParams(vmem_limit_bytes=4 * 2**20),
        name="pack",
    )(pltpu.with_memory_space_constraint(log_conf, pltpu.HBM))


def begin_kernel(
    cuts, f_ref, b_ref, r_ref, cols_ref, k_ref, out_ref, w_ref, pick_ref, *refs
):
    rows, ny = f_ref.shape[1], f_ref.shape[2]
    odd, gy = position()
    ty_ref, tz_ref = refs[-2:]
    step = 64

    @pl.when(pl.program_id(0) == 0)
    def _():
        nz = f_ref.shape[3]
        ty_ref[...] = band(ny)
        tz_ref[...] = band(nz)
        planes = pick_ref.shape[0]
        z = lax.broadcasted_iota(jnp.int32, (planes, nz), 1)
        k = lax.broadcasted_iota(jnp.int32, (planes, nz), 0)
        for piece, chosen in enumerate((lax.shift_right_logical(z + 2, 2) == k, z == 4 * k + 2)):
            value = jnp.where(chosen, 1.0, 0.0).astype(jnp.bfloat16)
            pick_ref[:, piece * nz : (piece + 1) * nz] = value
            pick_ref[:, (piece + 2) * nz : (piece + 3) * nz] = value
        tap = (lax.broadcasted_iota(jnp.int32, (NC, nz), 1) + 2) & 3
        for a in range(5):
            for b in range(5):
                taps = k_ref[a, b]
                near = jnp.broadcast_to(taps[:, 0:1], (NC, nz))
                for e in range(1, 4):
                    near = jnp.where(tap == e, taps[:, e : e + 1], near)
                w_ref[a, b, 0] = near
                w_ref[a, b, 1] = jnp.broadcast_to(taps[:, 4:5], (NC, nz))

    for (start, stop), first_ref, second_ref in zip(cuts, refs[0:-2:2], refs[1:-2:2]):
        first_ref[0] = f_ref[0, pl.ds(2 - 2 * odd, 2), start:stop]
        second_ref[0] = f_ref[0, pl.ds(2 * odd, 2), start:stop]
    for x in range(rows):
        plane = f_ref[0, x]
        for y in range(0, ny, step):
            ys = pl.ds(y, step)
            part = f_ref[0, x, ys]
            lap = jnp.dot(ty_ref[ys], plane, preferred_element_type=jnp.float32)
            lap += jnp.dot(part, tz_ref[...], preferred_element_type=jnp.float32)
            own = part.astype(jnp.float32)
            lap -= 30.0 * own
            for other in range(rows):
                if abs(other - x) == 1:
                    lap += 16.0 * f_ref[0, other, ys].astype(jnp.float32)
                elif abs(other - x) == 2:
                    lap -= f_ref[0, other, ys].astype(jnp.float32)
            rate = r_ref[x, ys].astype(jnp.float32)
            noise = b_ref[0, x, ys].astype(jnp.float32)
            out_ref[0, x, ys] = own - RELAX_STEP * rate * own + NOISE_AMP * noise + STENCIL * lap
        near_row = lax.broadcasted_iota(jnp.int32, (8, 1), 0)
        first = cols_ref[0, x, 0:1]
        second = cols_ref[0, x, 1:2]

        @pl.when(gy == 1)
        def _():
            extra = jnp.where(near_row == 0, 16.0 * second - first, jnp.where(near_row == 1, -second, 0.0))
            out_ref[0, x, 0:8] += STENCIL * extra

        @pl.when(gy == 0)
        def _():
            extra = jnp.where(near_row == 7, 16.0 * first - second, jnp.where(near_row == 6, -first, 0.0))
            out_ref[0, x, ny - 8 : ny] += STENCIL * extra


def begin(log_conf, brownian, relax_rate, cols, kernel, cuts):
    comps, rows, ny, nz = log_conf.shape
    whole = lambda *shape: pl.BlockSpec(shape, lambda c: (0,) * len(shape))
    block = pl.BlockSpec((1, rows, ny, nz), lambda c: (c, 0, 0, 0))
    heights = [stop - start for start, stop in cuts for _ in range(2)]
    return pl.pallas_call(
        functools.partial(begin_kernel, cuts),
        grid=(comps,),
        in_specs=[
            block,
            block,
            whole(rows, ny, nz),
            pl.BlockSpec((1, rows, 2, nz), lambda c: (c, 0, 0, 0)),
            whole(5, 5, comps, 5),
        ],
        out_specs=[block, whole(5, 5, 2, comps, nz), whole(nz // 4, 4 * nz)]
        + [pl.BlockSpec((1, 2, height, nz), lambda c: (c, 0, 0, 0)) for height in heights],
        out_shape=[
            jax.ShapeDtypeStruct((comps, rows, ny, nz), jnp.float32),
            jax.ShapeDtypeStruct((5, 5, 2, comps, nz), jnp.float32),
            jax.ShapeDtypeStruct((nz // 4, 4 * nz), jnp.bfloat16),
        ]
        + [jax.ShapeDtypeStruct((comps, 2, height, nz), log_conf.dtype) for height in heights],
        scratch_shapes=[pltpu.VMEM((ny, ny), jnp.bfloat16), pltpu.VMEM((nz, nz), jnp.bfloat16)],
        compiler_params=pltpu.CompilerParams(vmem_limit_bytes=16 * 2**20),
        cost_estimate=pl.CostEstimate(
            flops=30 * comps * rows * ny * nz, bytes_accessed=10 * comps * rows * ny * nz, transcendentals=0
        ),
        name="begin",
    )(*(pltpu.with_memory_space_constraint(x, pltpu.HBM) for x in (log_conf, brownian, relax_rate)), cols, jnp.transpose(kernel, (1, 2, 0, 3)))


def finish_kernel(start, stop, has_base, u_ref, a_ref, b_ref, w_ref, pick_ref, *refs):
    if has_base:
        base_ref, out_ref, stress, sums = refs
    else:
        out_ref, stress, sums = refs
    rows, ny, nz = u_ref.shape[1:]
    width, nj = stop - start, ny // 4
    own_j, planes, pieces = width // 4, out_ref.shape[0] // ROWS, nz // LANES
    first_ref, second_ref = (b_ref, a_ref) if 0 < start < 3 * u_ref.shape[2] // 4 else (a_ref, b_ref)
    odd, _ = position()
    compact = len(sums.shape) == 2
    if compact:
        for t in range(2):
            sums[t * nj + 8 * NC : (t + 1) * nj] = jnp.zeros((nj - 8 * NC, 2 * nz), jnp.float32)
    for c in range(NC):
        for r in range(rows):
            for piece in range(pieces):
                stress[c, r, piece, 0:LEAD] = jnp.zeros((LEAD, LANES), jnp.float32)
                stress[c, r, piece, LEAD + width :] = jnp.zeros((TAIL, LANES), jnp.float32)

    for side, halo_ref in enumerate((first_ref, second_ref)):
        upper = (odd == side).astype(jnp.int32)
        near, far = 1 - upper, upper
        edge, inner = 3 * upper, 1 + upper

        def chunk(step, carry, halo_ref=halo_ref, near=near, far=far, edge=edge, inner=inner):
            y = pl.multiple_of(step * 16, 16)
            ys, us = pl.ds(y, 16), pl.ds(start + y, 16)
            updated = ([], [])
            for c in range(NC):
                close = halo_ref[c, near, ys].astype(jnp.float32)
                distant = halo_ref[c, far, ys].astype(jnp.float32)
                updated[0].append(u_ref[c, inner, us] - STENCIL * close)
                updated[1].append(u_ref[c, edge, us] + (16.0 * STENCIL) * close - STENCIL * distant)
            for row, (xx, xy, xz, yy, yz, zz) in zip((inner, edge), updated):
                xy2, xz2, yz2 = xy * xy, xz * xz, yz * yz
                values = (
                    xx + 0.5 * (xx * xx + xy2 + xz2),
                    xy + 0.5 * (xy * (xx + yy) + xz * yz),
                    xz + 0.5 * (xz * (xx + zz) + xy * yz),
                    yy + 0.5 * (xy2 + yy * yy + yz2),
                    yz + 0.5 * (yz * (yy + zz) + xy * xz),
                    zz + 0.5 * (xz2 + yz2 + zz * zz),
                )
                for c in range(NC):
                    for piece in range(pieces):
                        lanes = slice(piece * LANES, (piece + 1) * LANES)
                        stress[c, row, piece, pl.ds(y + LEAD, 16)] = values[c][:, lanes]
            return carry

        lax.fori_loop(0, width // 16, chunk, 0)

    taps = {0: ((0, 2), (1, 3), (2, 4)), 1: ((2, 0), (3, 1))}
    for c in range(NC):
        for t in range(2):
            weight = {}
            for row, a in taps[t]:
                for b in range(5):
                    for k in range(2):
                        weight[row, b, k] = w_ref[a, b, k, c : c + 1]
            for jb in range(own_j // 8 + 1):
                total = [None, None]
                for b in range(5 if jb < own_j // 8 else 2):
                    at = pl.ds(LEAD + 32 * jb + b - 2, 8, stride=4)
                    for row, _ in taps[t]:
                        value = jnp.concatenate([stress[c, row, piece, at] for piece in range(pieces)], axis=1)
                        for k in range(2):
                            term = value * weight[row, b, k]
                            total[k] = term if total[k] is None else total[k] + term
                for k in range(2):
                    lanes = slice(k * nz, (k + 1) * nz)
                    if not compact:
                        sums[c, t, 8 * jb : 8 * jb + 8, lanes] = total[k]
                    elif jb == 0:
                        sums[t * nj + 8 * c : t * nj + 8 * c + 8, lanes] = total[k]
                    else:
                        at = t * nj + 8 * NC + c
                        sums[at : at + 1, lanes] = total[k][0:1]

    def reduced(values):
        high = values.astype(jnp.bfloat16)
        low = (values - high.astype(jnp.float32)).astype(jnp.bfloat16)
        both = jnp.concatenate([high, low], axis=1)
        return lax.dot_general(
            pick_ref[...], both, (((1,), (1,)), ((), ())), preferred_element_type=jnp.float32
        )

    def put(place, value):
        at = pl.ds(place, planes, stride=ROWS)
        if has_base:
            value = value + base_ref[at, :]
        out_ref[at, :] = value

    if compact:
        lane = lax.broadcasted_iota(jnp.int32, (planes, 2 * nj), 1)
        spread = reduced(sums[...])
        for c in range(NC):
            moved = pltpu.roll(spread, nj - 8 - 8 * c, 1)
            put(c, jnp.where((lane & (nj - 1)) >= nj - 8, moved, 0.0))
        out_ref[pl.ds(NC, planes, stride=ROWS), :] = spread
        return

    first_j = start // 4
    held = min(own_j + 8, nj - first_j)
    for c in range(NC):
        parts = []
        for t in range(2):
            if first_j:
                parts.append(jnp.zeros((first_j, 2 * nz), jnp.float32))
            parts.append(sums[c, t, 0:held])
            if first_j + held < nj:
                parts.append(jnp.zeros((nj - first_j - held, 2 * nz), jnp.float32))
        put(c, reduced(jnp.concatenate(parts, axis=0)))
    out_ref[pl.ds(NC, planes, stride=ROWS), :] = jnp.zeros((planes, 2 * nj), jnp.float32)


def finish(start, stop, begun, halos, weights, pick, base):
    comps, rows, ny, nz = begun.shape
    planes, nj = nz // 4, ny // 4
    places = (2 * nj, 2 * nz) if stop == ny else (comps, 2, (stop - start) // 4 + 8, 2 * nz)
    operands = [begun, *(halos[::-1] if 0 < start < 3 * begun.shape[2] // 4 else halos), weights, pick] + ([] if base is None else [base])
    operands = [pltpu.with_memory_space_constraint(x, pltpu.VMEM) for x in operands]
    return pl.pallas_call(
        functools.partial(finish_kernel, start, stop, base is not None),
        in_specs=[pl.BlockSpec(memory_space=pltpu.VMEM)] * len(operands),
        out_specs=pl.BlockSpec(memory_space=pltpu.VMEM),
        out_shape=jax.ShapeDtypeStruct((planes * ROWS, 2 * nj), jnp.float32),
        scratch_shapes=[
            pltpu.VMEM((comps, rows, nz // LANES, LEAD + stop - start + TAIL, LANES), jnp.float32),
            pltpu.VMEM(places, jnp.float32),
        ],
        compiler_params=pltpu.CompilerParams(vmem_limit_bytes=16 * 2**20),
        cost_estimate=pl.CostEstimate(
            flops=80 * comps * (stop - start) * nz, bytes_accessed=32 * comps * (stop - start) * nz, transcendentals=0
        ),
        name="finish",
    )(*operands)


def gather_kernel(in_ref, out_ref):
    count, lanes = out_ref.shape[2], out_ref.shape[3]
    half = lanes // 2
    lane = lax.broadcasted_iota(jnp.int32, (count, lanes), 1)
    row = lax.broadcasted_iota(jnp.int32, (count, lanes), 0)
    low = lane < half
    beyond = in_ref[pl.ds(NC, count, stride=2 * ROWS), :]
    for c in range(NC):
        first = in_ref[pl.ds(c, count, stride=2 * ROWS), :]
        second = in_ref[pl.ds(ROWS + c, count, stride=2 * ROWS), :]
        own = jnp.where(low, first, pltpu.roll(second, half, 1))
        own += jnp.where(lane == half, pltpu.roll(beyond, half - 8 * NC - c, 1), 0.0)
        after = jnp.where(low, pltpu.roll(first, half, 1), second)
        after += jnp.where(lane == half, pltpu.roll(beyond, lanes - 8 * NC - c, 1), 0.0)
        out_ref[c, 0] = own + jnp.where(row > 0, pltpu.roll(after, 1, 0), 0.0)


def local(log_conf, brownian, relax_rate, kernel):
    comps, rows, ny, nz = log_conf.shape
    width_gx, width_gy = lax.axis_size("gx"), lax.axis_size("gy")
    planes = nz // 4
    assert comps == NC and rows == 4 and width_gy == 2 and width_gx % 2 == 0
    assert planes == width_gx * width_gy and ny == 256

    swap_first = [(i, i ^ 1) for i in range(width_gx)]
    swap_second = [(i, ((i + 1) ^ 1) - 1) for i in range(1, width_gx - 1)]
    cuts = [(0, 5 * ny // 8), (5 * ny // 8, 7 * ny // 8), (7 * ny // 8, ny)]
    early = cuts[0][1]
    (first,) = pack(log_conf, early, False)
    second, cols = pack(log_conf, early, True)
    halos = [[lax.ppermute(first, "gx", swap_first), lax.ppermute(second, "gx", swap_second)]]
    cols = lax.ppermute(cols, "gy", [(0, 1), (1, 0)])
    begun, weights, pick, *sent = begin(log_conf, brownian, relax_rate, cols, kernel, cuts[1:])
    for first, second in zip(sent[0::2], sent[1::2]):
        halos.append([lax.ppermute(first, "gx", swap_first), lax.ppermute(second, "gx", swap_second)])

    part = None
    for (start, stop), pair in zip(cuts, halos):
        part = finish(start, stop, begun, pair, weights, pick, part)
    moved = lax.all_to_all(part.reshape(planes, 1, ROWS * ny // 2), ("gx", "gy"), 0, 0, tiled=True)
    return pl.pallas_call(
        gather_kernel,
        out_shape=jax.ShapeDtypeStruct((comps, 1, width_gx, ny // 2), jnp.float32),
        in_specs=[pl.BlockSpec(memory_space=pltpu.VMEM)],
        compiler_params=pltpu.CompilerParams(vmem_limit_bytes=4 * 2**20),
        name="gather",
    )(pltpu.with_memory_space_constraint(moved.reshape(planes * ROWS, ny // 2), pltpu.VMEM))


def solution(mesh):
    return jax.shard_map(
        local,
        mesh=mesh,
        in_specs=(
            P(None, ("grp", "gx"), "gy", None),
            P(None, ("grp", "gx"), "gy", None),
            P(("grp", "gx"), "gy", None),
            P(),
        ),
        out_specs=P(None, ("gx", "gy"), "grp", None),
        check_vma=False,
    )
```
